32 devices in a mesh: modes: 16 (over z, x, core), rad: 2 (over y).
Axes of the slice: x: 2, y: 2, z: 4, core: 2. Of those that a mesh axis runs over, the one named last changes fastest.
Arguments:
- forcing: bfloat16 [3, 1024, 256, 256], P(None, 'modes', 'rad'), may hold values from -6 to 6
- diffusion: float32 [3], replicated, may hold values from 0.05 to 1
- axial_forward: float32 [256, 256], replicated, may hold values from -0.375 to 0.375
- axial_inverse_map: float32 [256, 256], replicated, may hold values from -0.375 to 0.375
- axial_eigenvalues: float32 [256], replicated, may hold values from 0.05 to 10
- radial_forward: float32 [128, 256, 256], P(('modes', 'rad')), may hold values from -0.375 to 0.375
- radial_backward: float32 [128, 256, 256], P(('modes', 'rad')), may hold values from -0.375 to 0.375
- radial_eigenvalues: float32 [128, 256], P(('modes', 'rad')), may hold values from 0.05 to 10
Outputs:
- solution: float32 [3, 128, 2, 256, 256], P(None, 'modes', None, 'rad')
The draws below stay inside these ranges and needn't reach their ends.
All inputs are finite; a program needn't handle non-finite values.
Results may differ from the reference program's by a relative error of at most 0.0003.
Values may be sent and summed in bfloat16 or wider, within the bound.
No kernel may reach another device: no remote copies, remote signals or barrier semaphores. Data moves between devices by JAX's collectives and lax.ppermute only.
A program may use at most 128 MiB of HBM per device.

```python
import math
import jax
import jax.numpy as jnp
from jax import lax

FIELDS = 3
NT = 1024
NR = 256
NZ = 256
MODES = 128


def block_levels(stream_key, dims, split, smallest, high):
    gain, own = 1.0, jax.random.fold_in(stream_key, 6)
    for axis_at, shards_of in split:
        heights = jnp.exp(jax.random.uniform(jax.random.fold_in(own, axis_at), (shards_of,), jnp.float32, smallest / len(split), high / len(split)))
        gain = gain * jnp.repeat(heights, dims[axis_at] // shards_of).reshape([-1 if axis == axis_at else 1 for axis in range(len(dims))])
    return gain


def noise(stream_key, dims, width, bound, cuts=(), kind=jnp.bfloat16):
    gain = block_levels(stream_key, dims, cuts, -0.22, 0.18) if cuts else 1.0
    drawn = jax.random.normal(stream_key, dims, jnp.float32) * width * gain
    return jnp.minimum(jnp.maximum(drawn, -bound), bound).astype(kind)


def setup_inputs(seed: int = 0) -> dict:
    key_list = jax.random.split(jax.random.key(seed), 9)
    forcing = noise(key_list[0], (FIELDS, NT, NR, NZ), 1.0, 6.0, ((1, 16), (2, 2)))
    diffusion = jnp.clip(jnp.exp(jax.random.uniform(key_list[1], (FIELDS,), jnp.float32, math.log(0.05), math.log(1.0))), 0.05, 1.0)
    axial_forward = noise(key_list[2], (NZ, NZ), NZ ** -0.5, 0.375, (), jnp.float32)
    axial_inverse_map = noise(key_list[3], (NZ, NZ), NZ ** -0.5, 0.375, (), jnp.float32)
    axial_eigenvalues = jnp.clip(jnp.exp(jax.random.uniform(key_list[4], (NZ,), jnp.float32, math.log(0.05), math.log(10.0))), 0.05, 10.0)
    radial_forward = noise(key_list[5], (MODES, NR, NR), NR ** -0.5, 0.375, ((0, 32),), jnp.float32)
    radial_backward = noise(key_list[6], (MODES, NR, NR), NR ** -0.5, 0.375, ((0, 32),), jnp.float32)
    radial_eigenvalues = jnp.clip(jnp.exp(math.log(10.0) - 5.2983174 * jax.random.uniform(key_list[7], (MODES, NR), jnp.float32) ** block_levels(key_list[7], (MODES, NR), ((0, 32),), -0.2, 0.2)), 0.05, 10.0)
    return dict(forcing=forcing, diffusion=diffusion, axial_forward=axial_forward, axial_inverse_map=axial_inverse_map, axial_eigenvalues=axial_eigenvalues, radial_forward=radial_forward, radial_backward=radial_backward, radial_eigenvalues=radial_eigenvalues)


def azimuthal_part(field_values):
    spectrum = jnp.fft.rfft(field_values.astype(jnp.float32), axis=0)[:MODES] * (1.0 / math.sqrt(NT))
    return jnp.stack([jnp.real(spectrum), jnp.imag(spectrum)], axis=1)

def reference(forcing, diffusion, axial_forward, axial_inverse_map, axial_eigenvalues, radial_forward, radial_backward, radial_eigenvalues):
    spectrum = lax.map(azimuthal_part, forcing)
    by_mode = jnp.transpose(spectrum, (1, 0, 2, 3, 4))
    highest_mode = lax.Precision.HIGHEST

    def modal_solve(operands):
        spectral_coefficients, forward_map, backward, eigenvalues = operands
        axial_coef = jnp.einsum('fcrz,qz->fcrq', spectral_coefficients, axial_forward, precision=highest_mode)
        radial_coefficients = jnp.einsum('ir,fcrq->fciq', forward_map, axial_coef, precision=highest_mode)
        denominator = 1.0 + diffusion[:, None, None, None] * (eigenvalues[None, None, :, None] + axial_eigenvalues[None, None, None, :])
        scaled = radial_coefficients / denominator
        returned = jnp.einsum('ri,fciq->fcrq', backward, scaled, precision=highest_mode)
        return jnp.einsum('zq,fcrq->fcrz', axial_inverse_map, returned, precision=highest_mode)
    solved = lax.map(modal_solve, (by_mode, radial_forward, radial_backward, radial_eigenvalues))
    return jnp.transpose(solved, (1, 0, 2, 3, 4))
```

```python
import functools
import math

import jax
import jax.numpy as jnp
import numpy as np
from jax import lax
from jax.experimental import pallas as pl
from jax.experimental.pallas import tpu as pltpu
from jax.sharding import PartitionSpec as P

BF16 = jnp.bfloat16
F32 = jnp.float32
VMEM_BYTES = 48 * 1024 * 1024

CODE_SPAN = 126.0
CODE_MID = 0.5
LN2 = math.log(2.0)
DECODE_SLOPE = 1.0 / (LN2 * CODE_SPAN)
DECODE_SHIFT = CODE_MID / CODE_SPAN
TINY = 1e-35
LOG_BASE = 125.0
LOG_RANGE = 250.0
UNIT_PART = 2.0**-6


def code_scale(largest):
    return (largest * 1.008).astype(BF16).astype(F32)


def linear_encode(values, scale):
    inverse = jnp.where(scale > TINY, CODE_SPAN / jnp.maximum(scale, TINY), 0.0)
    return jnp.exp2(values * inverse + CODE_MID)


def linear_decode(coded, scale):
    return scale * (jnp.log(coded) * DECODE_SLOPE - DECODE_SHIFT)


def log_gain(bound):
    return LOG_RANGE / math.log2(1.0 + bound / UNIT_PART)


def log_encode(values, unit, gain):
    inverse = jnp.where(unit > TINY, 1.0 / jnp.maximum(unit, TINY), 0.0)
    magnitude = jnp.exp2(jnp.log(1.0 + jnp.abs(values) * inverse) * (gain / LN2) - LOG_BASE)
    return jnp.where(values < 0.0, -magnitude, magnitude)


def log_decode(coded, unit, gain):
    magnitude = jnp.exp2(jnp.log(jnp.abs(coded)) * (1.0 / (LN2 * gain)) + LOG_BASE / gain)
    magnitude = unit * (magnitude - 1.0)
    return jnp.where(coded < 0.0, -magnitude, magnitude)


def window_basis(window, total, retained, rank):
    points = np.arange(window)
    inner = np.arange(1, window)
    diagonal = np.cos(np.pi * (2 * points - window + 1) / total) * np.cos(
        np.pi * (2 * retained - 1) / total
    )
    beside = -np.sin(np.pi * inner / total) * np.sin(np.pi * (window - inner) / total)
    _, vectors = np.linalg.eigh(np.diag(diagonal) + np.diag(beside, 1) + np.diag(beside, -1))
    basis = vectors[:, :rank]
    signs = np.where(np.sum(basis * (points + 0.37)[:, None] ** 2, axis=0) < 0, -1.0, 1.0)
    return basis * signs


def mode_rows(total, retained):
    phase = np.arange(retained)[:, None] * np.arange(total)[None, :] % total
    radians = phase * (2.0 * np.pi / total)
    rows = np.stack([np.cos(radians), -np.sin(radians)], axis=1) / np.sqrt(total)
    return rows.reshape(2 * retained, total)


def halves(table):
    upper = table.astype(np.float32).astype(jnp.bfloat16)
    lower = (table - upper.astype(np.float64)).astype(np.float32).astype(jnp.bfloat16)
    return upper, lower


def split(values):
    upper = values.astype(BF16)
    return upper, (values - upper.astype(F32)).astype(BF16)


def dot3(left, right, contract=((1,), (0,))):
    dims = (contract, ((), ()))
    dot = functools.partial(lax.dot_general, dimension_numbers=dims, preferred_element_type=F32)
    return dot(left[0], right[0]) + (dot(left[0], right[1]) + dot(left[1], right[0]))


ROWS_BY_ROWS = ((1,), (1,))


def encode_body(upper_ref, lower_ref, forcing_ref, out_ref, *, group, kept):
    points, rows, width = forcing_ref.shape[1:]
    block = forcing_ref[0].astype(F32)
    for part in range(rows // group):
        piece = block[:, part * group : (part + 1) * group, :].reshape(points * group, width)
        piece = piece.astype(BF16)
        coefficients = jnp.dot(upper_ref[...], piece, preferred_element_type=F32)
        coefficients += jnp.dot(lower_ref[...], piece, preferred_element_type=F32)
        coefficients = coefficients.reshape(group, kept, width)
        scale = code_scale(jnp.max(jnp.abs(coefficients), axis=1, keepdims=True))
        coded = linear_encode(coefficients, scale)
        place = lax.broadcasted_iota(jnp.int32, coded.shape, 1)
        coded = jnp.where(place == kept - 1, scale, coded)
        out_ref[part] = coded.reshape(group * kept, width).astype(BF16)


def middle_body(
    unit_ref, table_upper_ref, table_lower_ref, axial_ref, in_ref, out_ref, *, kept, rows, gain, field
):
    sources, _, width = in_ref.shape
    axial = split(axial_ref[...])
    table = (table_upper_ref[...], table_lower_ref[...])
    owners = out_ref.shape[0]
    parts = []
    for row in range(rows):
        coded = in_ref[:, row * kept : (row + 1) * kept, :].astype(F32)
        values = linear_decode(coded, coded[:, kept - 1 : kept, :])
        place = lax.broadcasted_iota(jnp.int32, values.shape, 1)
        values = jnp.where(place == kept - 1, 0.0, values).reshape(sources * kept, width)
        spectrum = dot3(table, split(values))
        axial_coef = dot3(split(spectrum), axial, ROWS_BY_ROWS)
        coded = log_encode(axial_coef, unit_ref[field], gain)
        parts.append(coded.reshape(owners, -1, width))
    out_ref[...] = jnp.concatenate(parts, axis=1).astype(BF16)


def solve_body(
    place_ref,
    unit_ref,
    diffusion_ref,
    axial_eigen_ref,
    radial_eigen_ref,
    axial_ref,
    forward_ref,
    backward_ref,
    in_ref,
    *rest,
    gain,
    field,
    radial_devices,
):
    out_ref, send_ref, held_ref = rest[-3:]
    mode = pl.program_id(0)
    devices, rows, width = in_ref.shape
    per_group = devices // radial_devices
    stride = 2 * pl.num_programs(0)

    @pl.when(mode == 0)
    def _():
        for source in range(devices):
            target = (source % radial_devices) * per_group + source // radial_devices
            values = log_decode(in_ref[source].astype(F32), unit_ref[field], gain)
            for lane in range(width // 128):
                held_ref[lane, target * rows : (target + 1) * rows, :] = values[
                    :, lane * 128 : (lane + 1) * 128
                ]

    radial = devices * rows // stride
    pieces = []
    for part in range(2):
        for lane in range(width // 128):
            pieces.append(held_ref[lane, pl.ds(mode * 2 + part, radial, stride=stride), :])
    values = jnp.concatenate(pieces, axis=1)
    values = dot3(split(forward_ref[0]), split(values))
    eigen = jnp.broadcast_to(radial_eigen_ref[0], (128, radial)).T[:, :1]
    denominator = 1.0 + diffusion_ref[field] * (eigen + axial_eigen_ref[...])
    inverse = 1.0 / denominator
    values = jnp.concatenate([values[:, :width] * inverse, values[:, width:] * inverse], axis=1)
    values = dot3(split(backward_ref[0]), split(values))
    values = jnp.concatenate([values[:, :width], values[:, width:]], axis=0)
    values = dot3(split(values), split(axial_ref[...]), ROWS_BY_ROWS)
    values = values.reshape(2, radial_devices, radial // radial_devices, width)
    first = place_ref[0] == 0
    out_ref[0, 0] = jnp.where(first, values[:, 0], values[:, 1])
    other = jnp.where(first, values[:, 1], values[:, 0]).reshape(radial, width)
    scale = code_scale(jnp.max(jnp.abs(other), axis=0, keepdims=True))
    send_ref[0, :radial, :] = linear_encode(other, scale).astype(BF16)
    send_ref[0, radial:, :] = jnp.broadcast_to(scale, (16, width)).astype(BF16)


def finish_body(place_ref, in_ref, _, out_ref):
    radial, width = out_ref.shape[2] * out_ref.shape[3], out_ref.shape[4]
    coded = in_ref[0].astype(F32)
    values = linear_decode(coded[:radial], coded[radial : radial + 1])
    out_ref[0, 0] = values.reshape(out_ref.shape[2:])


def params():
    return pltpu.CompilerParams(
        vmem_limit_bytes=VMEM_BYTES, dimension_semantics=("arbitrary",)
    )


def whole(shape):
    return pl.BlockSpec(shape, lambda *_: (0,) * len(shape))


SMEM = pl.BlockSpec(memory_space=pltpu.SMEM)


def paired_plan(
    forcing,
    diffusion,
    axial_forward,
    axial_inverse_map,
    axial_eigenvalues,
    radial_forward,
    radial_backward,
    radial_eigenvalues,
):
    fields, slab, radial_block, width = forcing.shape
    processors, radial_devices = lax.axis_size("modes"), lax.axis_size("rad")
    devices = processors * radial_devices
    total, radial = slab * processors, radial_block * radial_devices
    own_modes = radial_forward.shape[0]
    retained = own_modes * devices
    group = radial_block // processors
    kept = slab // 2
    rank = kept - 1
    axes = ("modes", "rad")

    basis = window_basis(slab, total, retained, rank)
    spread = np.zeros((group, kept, slab, group))
    for row in range(group):
        spread[row, :rank, :, row] = basis.T
    spread_upper, spread_lower = halves(spread.reshape(group * kept, slab * group))
    combine = np.zeros((2 * retained, processors, kept))
    modes = mode_rows(total, retained).reshape(2 * retained, processors, slab)
    combine[:, :, :rank] = modes @ basis
    table_upper, table_lower = halves(combine.reshape(2 * retained, processors * kept))

    bound = math.sqrt(total) * 0.375 * width
    gain = log_gain(bound)
    largest = jnp.max(jnp.abs(forcing), axis=(1, 2, 3)).astype(F32)
    unit = lax.pmax(largest, axes) * UNIT_PART
    place = lax.axis_index("rad").astype(jnp.int32).reshape(1)
    axial_eigen = axial_eigenvalues.reshape(1, width)
    radial_eigen = radial_eigenvalues.reshape(own_modes, 1, radial)

    def encode(field):
        steps = processors // 2
        return pl.pallas_call(
            functools.partial(encode_body, group=group, kept=kept),
            grid=(steps,),
            in_specs=[
                whole(spread_upper.shape),
                whole(spread_lower.shape),
                pl.BlockSpec((1, slab, 2 * group, width), lambda i: (field, 0, i, 0)),
            ],
            out_specs=pl.BlockSpec((2, group * kept, width), lambda i: (i, 0, 0)),
            out_shape=jax.ShapeDtypeStruct((processors, group * kept, width), BF16),
            compiler_params=params(),
            name="window_coefficients",
        )(jnp.asarray(spread_upper), jnp.asarray(spread_lower), forcing)

    def middle(field, received):
        rows = 2
        per_owner = 2 * own_modes
        return pl.pallas_call(
            functools.partial(middle_body, kept=kept, rows=rows, gain=gain, field=field),
            grid=(group // rows,),
            in_specs=[
                SMEM,
                whole(table_upper.shape),
                whole(table_lower.shape),
                whole(axial_forward.shape),
                pl.BlockSpec((processors, rows * kept, width), lambda i: (0, i, 0)),
            ],
            out_specs=pl.BlockSpec((devices, rows * per_owner, width), lambda i: (0, i, 0)),
            out_shape=jax.ShapeDtypeStruct((devices, group * per_owner, width), BF16),
            compiler_params=params(),
            name="modal_axial_coefficients",
        )(unit, jnp.asarray(table_upper), jnp.asarray(table_lower), axial_forward, received)

    out_shape = jax.ShapeDtypeStruct((fields, own_modes * radial_devices, 2, radial_block, width), F32)
    out_block = (1, 1, 2, radial_block, width)
    send_rows = radial + 16

    def solve(field, received, out):
        carried = [] if out is None else [out]
        first = 9
        return pl.pallas_call(
            functools.partial(solve_body, gain=gain, field=field, radial_devices=radial_devices),
            grid_spec=pltpu.PrefetchScalarGridSpec(
                num_scalar_prefetch=1,
                grid=(own_modes,),
                in_specs=[
                    SMEM,
                    SMEM,
                    whole(axial_eigen.shape),
                    pl.BlockSpec((1, 1, radial), lambda i, _: (i, 0, 0)),
                    whole(axial_inverse_map.shape),
                    pl.BlockSpec((1, radial, radial), lambda i, _: (i, 0, 0)),
                    pl.BlockSpec((1, radial, radial), lambda i, _: (i, 0, 0)),
                    whole(received.shape),
                ]
                + [pl.BlockSpec(memory_space=pl.ANY) for _ in carried],
                out_specs=[
                    pl.BlockSpec(out_block, lambda i, y: (field, y[0] * own_modes + i, 0, 0, 0)),
                    pl.BlockSpec((1, send_rows, width), lambda i, _: (i, 0, 0)),
                ],
                scratch_shapes=[
                    pltpu.VMEM((width // 128, received.shape[0] * received.shape[1], 128), F32)
                ],
            ),
            out_shape=[out_shape, jax.ShapeDtypeStruct((own_modes, send_rows, width), BF16)],
            input_output_aliases={first: 0} if carried else {},
            compiler_params=params(),
            name="radial_solve",
        )(
            place,
            unit,
            diffusion,
            axial_eigen,
            radial_eigen,
            axial_inverse_map,
            radial_forward,
            radial_backward,
            received,
            *carried,
        )

    def finish(field, received, out):
        return pl.pallas_call(
            finish_body,
            grid_spec=pltpu.PrefetchScalarGridSpec(
                num_scalar_prefetch=1,
                grid=(own_modes,),
                in_specs=[
                    pl.BlockSpec((1, send_rows, width), lambda i, _: (i, 0, 0)),
                    pl.BlockSpec(memory_space=pl.ANY),
                ],
                out_specs=pl.BlockSpec(
                    out_block, lambda i, y: (field, (1 - y[0]) * own_modes + i, 0, 0, 0)
                ),
            ),
            out_shape=out_shape,
            input_output_aliases={2: 0},
            compiler_params=params(),
            name="partner_rows",
        )(place, received, out)

    def exchange(values, names):
        return lax.all_to_all(values, names, split_axis=0, concat_axis=0, tiled=True)

    windows = [exchange(encode(field), "modes") for field in range(fields)]
    spectra = [exchange(middle(field, windows[field]), axes) for field in range(fields)]
    out, sent = None, []
    for field in range(fields):
        out, send = solve(field, spectra[field], out)
        sent.append(lax.ppermute(send, "rad", [(0, 1), (1, 0)]))
        if field:
            out = finish(field - 1, sent[field - 1], out)
    return finish(fields - 1, sent[fields - 1], out)


def azimuthal_tables(retained, points):
    row_index = jnp.arange(2 * retained, dtype=jnp.int32)
    wavenumber = row_index // 2
    quarter = (row_index % 2).astype(jnp.float32) * (0.5 * math.pi)
    theta_index = jnp.arange(points, dtype=jnp.int32)
    phase_index = wavenumber[:, None] * theta_index[None, :] % points
    radians = phase_index.astype(jnp.float32) * (2.0 * math.pi / points) + quarter[:, None]
    table = jnp.cos(radians) * (1.0 / math.sqrt(points))
    upper = table.astype(jnp.bfloat16)
    widened = lax.optimization_barrier(upper).astype(jnp.float32)
    lower = (table - widened).astype(jnp.bfloat16)
    return (upper, lower)


def modal_solve(spectral_coefficients, forward_map, backward, eigenvalues, axial_part, diffusion):
    highest_mode = lax.Precision.HIGHEST
    radial_coefficients = jnp.einsum(
        "hzv,bhtvp->bhtzp", forward_map, spectral_coefficients, precision=highest_mode
    )
    denominator = 1.0 + diffusion[:, None, None, None, None] * (
        eigenvalues[None, :, None, :, None] + axial_part[None, None, None, None, :]
    )
    return jnp.einsum(
        "mri,fmciq->fmcrq", backward, radial_coefficients / denominator, precision=highest_mode
    )


def general_plan(
    forcing,
    diffusion,
    axial_forward,
    axial_inverse_map,
    axial_eigenvalues,
    radial_forward,
    radial_backward,
    radial_eigenvalues,
):
    highest_mode = lax.Precision.HIGHEST
    fields, slab_points, radial_block, axial_points = forcing.shape
    mode_processors = lax.axis_size("modes")
    radial_devices = lax.axis_size("rad")
    total_theta = slab_points * mode_processors
    retained = radial_forward.shape[0] * mode_processors * radial_devices
    table_upper, table_lower = azimuthal_tables(retained, total_theta)
    flat_values = forcing.reshape(fields, slab_points, radial_block * axial_points)
    columns = lax.all_to_all(flat_values, "modes", split_axis=2, concat_axis=1, tiled=True)
    first = jnp.einsum("kt,ftc->fkc", table_upper, columns, preferred_element_type=jnp.float32)
    second = jnp.einsum("kt,ftc->fkc", table_lower, columns, preferred_element_type=jnp.float32)
    spectral = lax.all_to_all(first + second, "modes", split_axis=1, concat_axis=2, tiled=True)
    local_modes = spectral.shape[1] // 2
    spectral = spectral.reshape(fields, local_modes, 2, radial_block, axial_points)
    axial_coef = jnp.einsum("fmcrz,qz->fmcrq", spectral, axial_forward, precision=highest_mode)
    exchanged = lax.all_to_all(axial_coef, "rad", split_axis=4, concat_axis=3, tiled=True)
    forward_rows, backward_rows, eigen_rows = (
        lax.all_gather(radial_forward, "rad", axis=0, tiled=True),
        lax.all_gather(radial_backward, "rad", axis=0, tiled=True),
        lax.all_gather(radial_eigenvalues, "rad", axis=0, tiled=True),
    )
    axial_block = axial_points // radial_devices
    axial_part = lax.dynamic_slice_in_dim(
        axial_eigenvalues, lax.axis_index("rad") * axial_block, axial_block
    )
    solved = modal_solve(exchanged, forward_rows, backward_rows, eigen_rows, axial_part, diffusion)
    returned = lax.all_to_all(solved, "rad", split_axis=3, concat_axis=4, tiled=True)
    return jnp.einsum("fmcrq,zq->fmcrz", returned, axial_inverse_map, precision=highest_mode)


def per_device(forcing, diffusion, axial_forward, *maps):
    processors, radial_devices = lax.axis_size("modes"), lax.axis_size("rad")
    _, slab, radial_block, width = forcing.shape
    own_modes = maps[2].shape[0]
    paired = (
        radial_devices == 2
        and radial_block == 8 * processors
        and width % 128 == 0
        and own_modes == 4
        and slab % 32 == 0
        and slab * processors == 8 * own_modes * processors * radial_devices
    )
    plan = paired_plan if paired else general_plan
    return plan(forcing, diffusion, axial_forward, *maps)


def solution(mesh):
    in_specs = (
        P(None, "modes", "rad", None),
        P(),
        P(),
        P(),
        P(),
        P(("modes", "rad"), None, None),
        P(("modes", "rad"), None, None),
        P(("modes", "rad"), None),
    )
    out_specs = P(None, "modes", None, "rad", None)
    return jax.shard_map(
        per_device, mesh=mesh, in_specs=in_specs, out_specs=out_specs, check_vma=False
    )
```

```python
import functools
import math

import jax
import jax.numpy as jnp
import numpy as np
from jax import lax
from jax.experimental import pallas as pl
from jax.experimental.pallas import tpu as pltpu
from jax.sharding import PartitionSpec as P

BF16 = jnp.bfloat16
F32 = jnp.float32
VMEM_BYTES = 60 * 1024 * 1024

CODE_SPAN = 126.0
CODE_MID = 0.5
LN2 = math.log(2.0)
DECODE_SLOPE = 1.0 / (LN2 * CODE_SPAN)
DECODE_SHIFT = CODE_MID / CODE_SPAN
TINY = 1e-35


def code_scale(largest):
    return (largest * 1.008).astype(BF16).astype(F32)


def linear_encode(values, scale):
    inverse = jnp.where(scale > TINY, CODE_SPAN / jnp.maximum(scale, TINY), 0.0)
    return jnp.exp2(values * inverse + CODE_MID)


def linear_decode(coded, scale):
    return scale * (jnp.log(coded) * DECODE_SLOPE - DECODE_SHIFT)


def window_basis(window, total, band, rank):
    points = np.arange(window)
    inner = np.arange(1, window)
    diagonal = np.cos(np.pi * (2 * points - window + 1) / total) * np.cos(np.pi * band / total)
    beside = -np.sin(np.pi * inner / total) * np.sin(np.pi * (window - inner) / total)
    _, vectors = np.linalg.eigh(np.diag(diagonal) + np.diag(beside, 1) + np.diag(beside, -1))
    basis = vectors[:, :rank]
    signs = np.where(np.sum(basis * (points + 0.37)[:, None] ** 2, axis=0) < 0, -1.0, 1.0)
    return basis * signs


def waves(modes, points, total):
    return np.exp(-2j * np.pi * (modes[:, None] * points[None, :] % total) / total)


def interleave(values):
    return np.stack([values.real, values.imag], axis=1).reshape(-1, values.shape[-1])


def half_tables(total, retained, slab, basis, sent):
    half, own = total // 2, retained // 2
    rank = basis.shape[1]
    envelope = window_basis(half, total, own, (sent - 1) // 2)
    local, join = [], []
    for side in range(2):
        points = side * half + np.arange(half)
        away = (1 - side) * own + np.arange(own)
        centre = (1 - side) * own + 0.5 * (own - 1)
        direct = waves(side * own + np.arange(own), points, total) / np.sqrt(total)
        carried = np.exp(-2j * np.pi * centre * points / total)[None, :] * envelope.T
        rows = np.concatenate([interleave(direct), interleave(carried)])
        rows = rows.reshape(rows.shape[0], -1, slab) @ basis
        table = np.zeros((2 * own + sent, half // slab, rank + 1))
        table[: rows.shape[0], :, :rank] = rows
        local.append(table.reshape(table.shape[0], -1))
        offsets = np.exp(-2j * np.pi * (away - centre)[:, None] * points[None, :] / total)
        weights = (offsets @ envelope) / np.sqrt(total)
        parts = np.zeros((own, 2, sent))
        count = 2 * weights.shape[1]
        parts[:, 0, 0:count:2], parts[:, 0, 1:count:2] = weights.real, -weights.imag
        parts[:, 1, 0:count:2], parts[:, 1, 1:count:2] = weights.imag, weights.real
        join.append(parts.reshape(2 * own, sent))
    return np.stack(local), np.stack(join[::-1])


def halves(table):
    upper = table.astype(np.float32).astype(jnp.bfloat16)
    lower = (table - upper.astype(np.float64)).astype(np.float32).astype(jnp.bfloat16)
    return upper, lower


def split(values):
    upper = values.astype(BF16)
    return upper, (values - upper.astype(F32)).astype(BF16)


def dot3(left, right, contract=((1,), (0,))):
    dims = (contract, ((), ()))
    dot = functools.partial(lax.dot_general, dimension_numbers=dims, preferred_element_type=F32)
    return dot(left[0], right[0]) + (dot(left[0], right[1]) + dot(left[1], right[0]))


ROWS_BY_ROWS = ((1,), (1,))


def encode_columns(values, kept):
    scale = code_scale(jnp.max(jnp.abs(values), axis=1, keepdims=True))
    place = lax.broadcasted_iota(jnp.int32, values.shape, 1)
    return jnp.where(place == kept - 1, scale, linear_encode(values, scale))


def decode_columns(coded, kept):
    values = linear_decode(coded, coded[:, kept - 1 : kept, :])
    place = lax.broadcasted_iota(jnp.int32, values.shape, 1)
    return jnp.where(place == kept - 1, 0.0, values)


def encode_body(upper_ref, lower_ref, forcing_ref, out_ref, *, group, kept):
    points, rows, width = forcing_ref.shape[1:]
    block = forcing_ref[0].astype(F32)
    for part in range(rows // group):
        piece = block[:, part * group : (part + 1) * group, :].reshape(points * group, width)
        piece = piece.astype(BF16)
        coefficients = jnp.dot(upper_ref[...], piece, preferred_element_type=F32)
        coefficients += jnp.dot(lower_ref[...], piece, preferred_element_type=F32)
        coded = encode_columns(coefficients.reshape(group, kept, width), kept)
        place = part * group * kept
        out_ref[0, place : place + group * kept, :] = coded.reshape(group * kept, width).astype(BF16)


def gather_body(_, upper_ref, lower_ref, in_ref, own_ref, send_ref, *, kept, sent, rows):
    sources, _, width = in_ref.shape
    table = (upper_ref[0], lower_ref[0])
    own = own_ref.shape[1]
    for row in range(rows):
        coded = in_ref[:, row * kept : (row + 1) * kept, :].astype(F32)
        values = decode_columns(coded, kept).reshape(sources * kept, width)
        sums = dot3(table, split(values))
        own_ref[row] = sums[:own]
        send_ref[row * sent : (row + 1) * sent, :] = encode_columns(sums[None, own:], sent)[0].astype(BF16)


def join_body(_, upper_ref, lower_ref, axial_ref, own_ref, in_ref, out_ref, held_ref, *, sent, rows):
    step = pl.program_id(0)
    width = in_ref.shape[1]
    owners, coded_rows = out_ref.shape[:2]
    block = coded_rows - 16
    table = (upper_ref[0], lower_ref[0])
    axial = split(axial_ref[...])
    for row in range(rows):
        coded = in_ref[row * sent : (row + 1) * sent, :].astype(F32)
        values = decode_columns(coded[None], sent)[0]
        spectrum = own_ref[row] + dot3(table, split(values))
        axial_coef = dot3(split(spectrum), axial, ROWS_BY_ROWS).reshape(owners, -1, width)
        each = axial_coef.shape[1]
        place = pl.multiple_of((step * rows + row) * each, each)
        held_ref[:, pl.ds(place, each), :] = axial_coef

    @pl.when(step == pl.num_programs(0) - 1)
    def _():
        for owner in range(owners):
            values = held_ref[owner]
            scale = code_scale(jnp.max(jnp.abs(values), axis=0, keepdims=True))
            out_ref[owner, :block, :] = linear_encode(values, scale).astype(BF16)
            out_ref[owner, block:, :] = jnp.broadcast_to(scale, (16, width)).astype(BF16)


def solve_body(
    place_ref,
    diffusion_ref,
    axial_eigen_ref,
    radial_eigen_ref,
    axial_ref,
    forward_ref,
    backward_ref,
    in_ref,
    *rest,
    field,
    radial_devices,
):
    out_ref, send_ref, held_ref = rest[-3:]
    mode = pl.program_id(0)
    devices, coded_rows, width = in_ref.shape
    rows = coded_rows - 16
    per_group = devices // radial_devices
    stride = 2 * pl.num_programs(0)

    @pl.when(mode == 0)
    def _():
        for source in range(devices):
            target = (source % radial_devices) * per_group + source // radial_devices
            coded = in_ref[source].astype(F32)
            values = linear_decode(coded[:rows], coded[rows : rows + 1])
            for lane in range(width // 128):
                held_ref[lane, target * rows : (target + 1) * rows, :] = values[
                    :, lane * 128 : (lane + 1) * 128
                ]

    radial = devices * rows // stride
    pieces = []
    for part in range(2):
        for lane in range(width // 128):
            pieces.append(held_ref[lane, pl.ds(mode * 2 + part, radial, stride=stride), :])
    values = jnp.concatenate(pieces, axis=1)
    values = dot3(split(forward_ref[0]), split(values))
    eigen = jnp.broadcast_to(radial_eigen_ref[0], (128, radial)).T[:, :1]
    denominator = 1.0 + diffusion_ref[field] * (eigen + axial_eigen_ref[...])
    inverse = 1.0 / denominator
    values = jnp.concatenate([values[:, :width] * inverse, values[:, width:] * inverse], axis=1)
    values = dot3(split(backward_ref[0]), split(values))
    values = jnp.concatenate([values[:, :width], values[:, width:]], axis=0)
    values = dot3(split(values), split(axial_ref[...]), ROWS_BY_ROWS)
    values = values.reshape(2, radial_devices, radial // radial_devices, width)
    first = place_ref[0] == 0
    out_ref[0, 0] = jnp.where(first, values[:, 0], values[:, 1])
    other = jnp.where(first, values[:, 1], values[:, 0]).reshape(radial, width)
    scale = code_scale(jnp.max(jnp.abs(other), axis=0, keepdims=True))
    send_ref[0, :radial, :] = linear_encode(other, scale).astype(BF16)
    send_ref[0, radial:, :] = jnp.broadcast_to(scale, (16, width)).astype(BF16)


def finish_body(place_ref, in_ref, _, out_ref):
    radial, width = out_ref.shape[2] * out_ref.shape[3], out_ref.shape[4]
    coded = in_ref[0].astype(F32)
    values = linear_decode(coded[:radial], coded[radial : radial + 1])
    out_ref[0, 0] = values.reshape(out_ref.shape[2:])


def params():
    return pltpu.CompilerParams(
        vmem_limit_bytes=VMEM_BYTES, dimension_semantics=("arbitrary",)
    )


def cost(microseconds):
    return pl.CostEstimate(
        flops=int(microseconds * 3e8), bytes_accessed=int(microseconds * 3e6), transcendentals=0
    )


def whole(shape):
    return pl.BlockSpec(shape, lambda *_: (0,) * len(shape))


SMEM = pl.BlockSpec(memory_space=pltpu.SMEM)


def paired_plan(
    forcing,
    diffusion,
    axial_forward,
    axial_inverse_map,
    axial_eigenvalues,
    radial_forward,
    radial_backward,
    radial_eigenvalues,
):
    fields, slab, radial_block, width = forcing.shape
    processors, radial_devices = lax.axis_size("modes"), lax.axis_size("rad")
    devices = processors * radial_devices
    total, radial = slab * processors, radial_block * radial_devices
    own_modes = radial_forward.shape[0]
    retained = own_modes * devices
    near = processors // 2
    owners = near * radial_devices
    rows = radial_block // near
    group, kept, sent = 8, slab // 2, 96
    per_owner = 2 * own_modes
    side = lax.axis_index("modes") // near
    place = jnp.stack([lax.axis_index("rad"), side]).astype(jnp.int32)

    basis = window_basis(slab, total, 2 * retained - 1, kept - 1)
    spread = np.zeros((group, kept, slab, group))
    for row in range(group):
        spread[row, : kept - 1, :, row] = basis.T
    spread_upper, spread_lower = halves(spread.reshape(group * kept, slab * group))
    local, join_table = half_tables(total, retained, slab, basis, sent)
    local_upper, local_lower = halves(local)
    join_upper, join_lower = halves(join_table)
    axial_eigen = axial_eigenvalues.reshape(1, width)
    radial_eigen = radial_eigenvalues.reshape(own_modes, 1, radial)

    def of_side(table):
        return pl.BlockSpec((1,) + table.shape[1:], lambda i, p: (p[1], 0, 0))

    def encode(field):
        return pl.pallas_call(
            functools.partial(encode_body, group=group, kept=kept),
            grid=(near,),
            in_specs=[
                whole(spread_upper.shape),
                whole(spread_lower.shape),
                pl.BlockSpec((1, slab, rows, width), lambda i: (field, 0, i, 0)),
            ],
            out_specs=pl.BlockSpec((1, rows * kept, width), lambda i: (i, 0, 0)),
            out_shape=jax.ShapeDtypeStruct((near, rows * kept, width), BF16),
            compiler_params=params(),
            cost_estimate=cost(7),
            name="window_coefficients",
        )(jnp.asarray(spread_upper), jnp.asarray(spread_lower), forcing)

    def gather(received):
        step = 2
        return pl.pallas_call(
            functools.partial(gather_body, kept=kept, sent=sent, rows=step),
            grid_spec=pltpu.PrefetchScalarGridSpec(
                num_scalar_prefetch=1,
                grid=(rows // step,),
                in_specs=[
                    of_side(local_upper),
                    of_side(local_lower),
                    pl.BlockSpec((near, step * kept, width), lambda i, _: (0, i, 0)),
                ],
                out_specs=[
                    pl.BlockSpec((step, retained, width), lambda i, _: (i, 0, 0)),
                    pl.BlockSpec((step * sent, width), lambda i, _: (i, 0)),
                ],
            ),
            out_shape=[
                jax.ShapeDtypeStruct((rows, retained, width), F32),
                jax.ShapeDtypeStruct((rows * sent, width), BF16),
            ],
            compiler_params=params(),
            cost_estimate=cost(5),
            name="half_sums",
        )(place, jnp.asarray(local_upper), jnp.asarray(local_lower), received)

    def join(own, received):
        step = 2
        block = rows * per_owner
        return pl.pallas_call(
            functools.partial(join_body, sent=sent, rows=step),
            grid_spec=pltpu.PrefetchScalarGridSpec(
                num_scalar_prefetch=1,
                grid=(rows // step,),
                in_specs=[
                    of_side(join_upper),
                    of_side(join_lower),
                    whole(axial_forward.shape),
                    pl.BlockSpec((step, retained, width), lambda i, _: (i, 0, 0)),
                    pl.BlockSpec((step * sent, width), lambda i, _: (i, 0)),
                ],
                out_specs=whole((owners, block + 16, width)),
                scratch_shapes=[pltpu.VMEM((owners, block, width), F32)],
            ),
            out_shape=jax.ShapeDtypeStruct((owners, block + 16, width), BF16),
            compiler_params=params(),
            cost_estimate=cost(6),
            name="modal_axial_coefficients",
        )(place, jnp.asarray(join_upper), jnp.asarray(join_lower), axial_forward, own, received)

    out_shape = jax.ShapeDtypeStruct((fields, own_modes * radial_devices, 2, radial_block, width), F32)
    out_block = (1, 1, 2, radial_block, width)
    send_rows = radial + 16

    def solve(field, received, out):
        carried = [] if out is None else [out]
        first = 8
        return pl.pallas_call(
            functools.partial(solve_body, field=field, radial_devices=radial_devices),
            grid_spec=pltpu.PrefetchScalarGridSpec(
                num_scalar_prefetch=1,
                grid=(own_modes,),
                in_specs=[
                    SMEM,
                    whole(axial_eigen.shape),
                    pl.BlockSpec((1, 1, radial), lambda i, _: (i, 0, 0)),
                    whole(axial_inverse_map.shape),
                    pl.BlockSpec((1, radial, radial), lambda i, _: (i, 0, 0)),
                    pl.BlockSpec((1, radial, radial), lambda i, _: (i, 0, 0)),
                    whole(received.shape),
                ]
                + [pl.BlockSpec(memory_space=pl.ANY) for _ in carried],
                out_specs=[
                    pl.BlockSpec(out_block, lambda i, y: (field, y[0] * own_modes + i, 0, 0, 0)),
                    pl.BlockSpec((1, send_rows, width), lambda i, _: (i, 0, 0)),
                ],
                scratch_shapes=[
                    pltpu.VMEM((width // 128, radial * per_owner, 128), F32)
                ],
            ),
            out_shape=[out_shape, jax.ShapeDtypeStruct((own_modes, send_rows, width), BF16)],
            input_output_aliases={first: 0} if carried else {},
            compiler_params=params(),
            cost_estimate=cost(7),
            name="radial_solve",
        )(
            place,
            diffusion,
            axial_eigen,
            radial_eigen,
            axial_inverse_map,
            radial_forward,
            radial_backward,
            received,
            *carried,
        )

    def finish(field, received, out):
        return pl.pallas_call(
            finish_body,
            grid_spec=pltpu.PrefetchScalarGridSpec(
                num_scalar_prefetch=1,
                grid=(own_modes,),
                in_specs=[
                    pl.BlockSpec((1, send_rows, width), lambda i, _: (i, 0, 0)),
                    pl.BlockSpec(memory_space=pl.ANY),
                ],
                out_specs=pl.BlockSpec(
                    out_block, lambda i, y: (field, (1 - y[0]) * own_modes + i, 0, 0, 0)
                ),
            ),
            out_shape=out_shape,
            input_output_aliases={2: 0},
            compiler_params=params(),
            cost_estimate=cost(2),
            name="partner_rows",
        )(place, received, out)

    sides = [list(range(near)), list(range(near, processors))]
    side_owners = [
        [m * radial_devices + y for m in members for y in range(radial_devices)] for members in sides
    ]

    def exchange(values, names, groups):
        return lax.all_to_all(
            values, names, split_axis=0, concat_axis=0, tiled=True, axis_index_groups=groups
        )

    def across(values):
        return lax.ppermute(values, "modes", [(i, (i + near) % processors) for i in range(processors)])

    windows = [exchange(encode(field), "modes", sides) for field in range(fields)]
    halves_of = [gather(windows[field]) for field in range(fields)]
    spectra = [
        exchange(join(own, across(send)), ("modes", "rad"), side_owners) for own, send in halves_of
    ]
    out, sent_rows = None, []
    for field in range(fields):
        out, send = solve(field, spectra[field], out)
        sent_rows.append(lax.ppermute(send, "rad", [(0, 1), (1, 0)]))
        if field:
            out = finish(field - 1, sent_rows[field - 1], out)
    return finish(fields - 1, sent_rows[fields - 1], out)


def azimuthal_tables(retained, points):
    row_index = jnp.arange(2 * retained, dtype=jnp.int32)
    wavenumber = row_index // 2
    quarter = (row_index % 2).astype(jnp.float32) * (0.5 * math.pi)
    theta_index = jnp.arange(points, dtype=jnp.int32)
    phase_index = wavenumber[:, None] * theta_index[None, :] % points
    radians = phase_index.astype(jnp.float32) * (2.0 * math.pi / points) + quarter[:, None]
    table = jnp.cos(radians) * (1.0 / math.sqrt(points))
    upper = table.astype(jnp.bfloat16)
    widened = lax.optimization_barrier(upper).astype(jnp.float32)
    lower = (table - widened).astype(jnp.bfloat16)
    return (upper, lower)


def modal_solve(spectral_coefficients, forward_map, backward, eigenvalues, axial_part, diffusion):
    highest_mode = lax.Precision.HIGHEST
    radial_coefficients = jnp.einsum(
        "hzv,bhtvp->bhtzp", forward_map, spectral_coefficients, precision=highest_mode
    )
    denominator = 1.0 + diffusion[:, None, None, None, None] * (
        eigenvalues[None, :, None, :, None] + axial_part[None, None, None, None, :]
    )
    return jnp.einsum(
        "mri,fmciq->fmcrq", backward, radial_coefficients / denominator, precision=highest_mode
    )


def general_plan(
    forcing,
    diffusion,
    axial_forward,
    axial_inverse_map,
    axial_eigenvalues,
    radial_forward,
    radial_backward,
    radial_eigenvalues,
):
    highest_mode = lax.Precision.HIGHEST
    fields, slab_points, radial_block, axial_points = forcing.shape
    mode_processors = lax.axis_size("modes")
    radial_devices = lax.axis_size("rad")
    total_theta = slab_points * mode_processors
    retained = radial_forward.shape[0] * mode_processors * radial_devices
    table_upper, table_lower = azimuthal_tables(retained, total_theta)
    flat_values = forcing.reshape(fields, slab_points, radial_block * axial_points)
    columns = lax.all_to_all(flat_values, "modes", split_axis=2, concat_axis=1, tiled=True)
    first = jnp.einsum("kt,ftc->fkc", table_upper, columns, preferred_element_type=jnp.float32)
    second = jnp.einsum("kt,ftc->fkc", table_lower, columns, preferred_element_type=jnp.float32)
    spectral = lax.all_to_all(first + second, "modes", split_axis=1, concat_axis=2, tiled=True)
    local_modes = spectral.shape[1] // 2
    spectral = spectral.reshape(fields, local_modes, 2, radial_block, axial_points)
    axial_coef = jnp.einsum("fmcrz,qz->fmcrq", spectral, axial_forward, precision=highest_mode)
    exchanged = lax.all_to_all(axial_coef, "rad", split_axis=4, concat_axis=3, tiled=True)
    forward_rows, backward_rows, eigen_rows = (
        lax.all_gather(radial_forward, "rad", axis=0, tiled=True),
        lax.all_gather(radial_backward, "rad", axis=0, tiled=True),
        lax.all_gather(radial_eigenvalues, "rad", axis=0, tiled=True),
    )
    axial_block = axial_points // radial_devices
    axial_part = lax.dynamic_slice_in_dim(
        axial_eigenvalues, lax.axis_index("rad") * axial_block, axial_block
    )
    solved = modal_solve(exchanged, forward_rows, backward_rows, eigen_rows, axial_part, diffusion)
    returned = lax.all_to_all(solved, "rad", split_axis=3, concat_axis=4, tiled=True)
    return jnp.einsum("fmcrq,zq->fmcrz", returned, axial_inverse_map, precision=highest_mode)


def per_device(forcing, diffusion, axial_forward, *maps):
    processors, radial_devices = lax.axis_size("modes"), lax.axis_size("rad")
    _, slab, radial_block, width = forcing.shape
    own_modes = maps[2].shape[0]
    paired = (
        radial_devices == 2
        and processors % 2 == 0
        and radial_block == 8 * processors
        and width % 128 == 0
        and own_modes == 4
        and slab % 32 == 0
        and slab * processors == 8 * own_modes * processors * radial_devices
    )
    plan = paired_plan if paired else general_plan
    return plan(forcing, diffusion, axial_forward, *maps)


def solution(mesh):
    in_specs = (
        P(None, "modes", "rad", None),
        P(),
        P(),
        P(),
        P(),
        P(("modes", "rad"), None, None),
        P(("modes", "rad"), None, None),
        P(("modes", "rad"), None),
    )
    out_specs = P(None, "modes", None, "rad", None)
    return jax.shard_map(
        per_device, mesh=mesh, in_specs=in_specs, out_specs=out_specs, check_vma=False
    )
```

```python
import functools
import math

import jax
import jax.numpy as jnp
import numpy as np
from jax import lax
from jax.experimental import pallas as pl
from jax.experimental.pallas import tpu as pltpu
from jax.sharding import PartitionSpec as P

BF16 = jnp.bfloat16
F32 = jnp.float32
VMEM_BYTES = 60 * 1024 * 1024

CODE_SPAN = 126.0
CODE_MID = 0.5
LN2 = math.log(2.0)
DECODE_SLOPE = 1.0 / (LN2 * CODE_SPAN)
DECODE_SHIFT = CODE_MID / CODE_SPAN
TINY = 1e-35


def code_scale(largest):
    return (largest * 1.008).astype(BF16).astype(F32)


def linear_encode(values, scale):
    inverse = jnp.where(scale > TINY, CODE_SPAN / jnp.maximum(scale, TINY), 0.0)
    return jnp.exp2(values * inverse + CODE_MID)


def linear_decode(coded, scale):
    return scale * (jnp.log(coded) * DECODE_SLOPE - DECODE_SHIFT)


def window_basis(window, total, band, rank):
    points = np.arange(window)
    inner = np.arange(1, window)
    diagonal = np.cos(np.pi * (2 * points - window + 1) / total) * np.cos(np.pi * band / total)
    beside = -np.sin(np.pi * inner / total) * np.sin(np.pi * (window - inner) / total)
    _, vectors = np.linalg.eigh(np.diag(diagonal) + np.diag(beside, 1) + np.diag(beside, -1))
    basis = vectors[:, :rank]
    signs = np.where(np.sum(basis * (points + 0.37)[:, None] ** 2, axis=0) < 0, -1.0, 1.0)
    return basis * signs


def waves(modes, points, total):
    return np.exp(-2j * np.pi * (modes[:, None] * points[None, :] % total) / total)


def interleave(values):
    return np.stack([values.real, values.imag], axis=1).reshape(-1, values.shape[-1])


def half_tables(total, retained, slab, basis, sent):
    half, own = total // 2, retained // 2
    rank = basis.shape[1]
    envelope = window_basis(half, total, own, (sent - 1) // 2)
    local, join = [], []
    for side in range(2):
        points = side * half + np.arange(half)
        away = (1 - side) * own + np.arange(own)
        centre = (1 - side) * own + 0.5 * (own - 1)
        direct = waves(side * own + np.arange(own), points, total) / np.sqrt(total)
        carried = np.exp(-2j * np.pi * centre * points / total)[None, :] * envelope.T
        rows = np.concatenate([interleave(direct), interleave(carried)])
        rows = rows.reshape(rows.shape[0], -1, slab) @ basis
        table = np.zeros((2 * own + sent, half // slab, rank + 1))
        table[: rows.shape[0], :, :rank] = rows
        local.append(table.reshape(table.shape[0], -1))
        offsets = np.exp(-2j * np.pi * (away - centre)[:, None] * points[None, :] / total)
        weights = (offsets @ envelope) / np.sqrt(total)
        parts = np.zeros((own, 2, sent))
        count = 2 * weights.shape[1]
        parts[:, 0, 0:count:2], parts[:, 0, 1:count:2] = weights.real, -weights.imag
        parts[:, 1, 0:count:2], parts[:, 1, 1:count:2] = weights.imag, weights.real
        join.append(parts.reshape(2 * own, sent))
    return np.stack(local), np.stack(join[::-1])


def halves(table):
    upper = table.astype(np.float32).astype(jnp.bfloat16)
    lower = (table - upper.astype(np.float64)).astype(np.float32).astype(jnp.bfloat16)
    return upper, lower


def split(values):
    upper = values.astype(BF16)
    return upper, (values - upper.astype(F32)).astype(BF16)


def dot3(left, right, contract=((1,), (0,))):
    dims = (contract, ((), ()))
    dot = functools.partial(lax.dot_general, dimension_numbers=dims, preferred_element_type=F32)
    return dot(left[0], right[0]) + (dot(left[0], right[1]) + dot(left[1], right[0]))


ROWS_BY_ROWS = ((1,), (1,))


def encode_columns(values, kept):
    scale = code_scale(jnp.max(jnp.abs(values), axis=1, keepdims=True))
    place = lax.broadcasted_iota(jnp.int32, values.shape, 1)
    return jnp.where(place == kept - 1, scale, linear_encode(values, scale))


def decode_columns(coded, kept):
    values = linear_decode(coded, coded[:, kept - 1 : kept, :])
    place = lax.broadcasted_iota(jnp.int32, values.shape, 1)
    return jnp.where(place == kept - 1, 0.0, values)


def encode_body(upper_ref, lower_ref, forcing_ref, _, out_ref, *, group, kept):
    points, rows, width = forcing_ref.shape[1:]
    block = forcing_ref[0].astype(F32)
    for part in range(rows // group):
        piece = block[:, part * group : (part + 1) * group, :].reshape(points * group, width)
        piece = piece.astype(BF16)
        coefficients = jnp.dot(upper_ref[...], piece, preferred_element_type=F32)
        coefficients += jnp.dot(lower_ref[...], piece, preferred_element_type=F32)
        coded = encode_columns(coefficients.reshape(group, kept, width), kept)
        place = part * group * kept
        out_ref[0, place : place + group * kept, :] = coded.reshape(group * kept, width).astype(BF16)


def gather_body(_, upper_ref, lower_ref, in_ref, __, own_ref, send_ref, *, kept, sent, rows):
    sources, _, width = in_ref.shape
    table = (upper_ref[0], lower_ref[0])
    own = own_ref.shape[1]
    for row in range(rows):
        coded = in_ref[:, row * kept : (row + 1) * kept, :].astype(F32)
        values = decode_columns(coded, kept).reshape(sources * kept, width)
        sums = dot3(table, split(values))
        own_ref[row] = sums[:own]
        send_ref[row * sent : (row + 1) * sent, :] = encode_columns(sums[None, own:], sent)[0].astype(BF16)


def join_body(
    _, upper_ref, lower_ref, axial_ref, own_ref, in_ref, __, out_ref, held_ref, *, sent, rows
):
    step = pl.program_id(0)
    width = in_ref.shape[1]
    owners, coded_rows = out_ref.shape[:2]
    block = coded_rows - 16
    table = (upper_ref[0], lower_ref[0])
    axial = split(axial_ref[...])
    for row in range(rows):
        coded = in_ref[row * sent : (row + 1) * sent, :].astype(F32)
        values = decode_columns(coded[None], sent)[0]
        spectrum = own_ref[row] + dot3(table, split(values))
        axial_coef = dot3(split(spectrum), axial, ROWS_BY_ROWS).reshape(owners, -1, width)
        each = axial_coef.shape[1]
        place = pl.multiple_of((step * rows + row) * each, each)
        held_ref[:, pl.ds(place, each), :] = axial_coef

    @pl.when(step == pl.num_programs(0) - 1)
    def _():
        for owner in range(owners):
            values = held_ref[owner]
            scale = code_scale(jnp.max(jnp.abs(values), axis=0, keepdims=True))
            out_ref[owner, :block, :] = linear_encode(values, scale).astype(BF16)
            out_ref[owner, block:, :] = jnp.broadcast_to(scale, (16, width)).astype(BF16)


def solve_body(
    place_ref,
    diffusion_ref,
    axial_eigen_ref,
    radial_eigen_ref,
    axial_ref,
    forward_ref,
    backward_ref,
    in_ref,
    *rest,
    field,
    radial_devices,
):
    out_ref, send_ref, held_ref = rest[-3:]
    mode = pl.program_id(0)
    devices, coded_rows, width = in_ref.shape
    rows = coded_rows - 16
    per_group = devices // radial_devices
    stride = 2 * pl.num_programs(0)

    @pl.when(mode == 0)
    def _():
        for source in range(devices):
            target = (source % radial_devices) * per_group + source // radial_devices
            coded = in_ref[source].astype(F32)
            values = linear_decode(coded[:rows], coded[rows : rows + 1])
            for lane in range(width // 128):
                held_ref[lane, target * rows : (target + 1) * rows, :] = values[
                    :, lane * 128 : (lane + 1) * 128
                ]

    radial = devices * rows // stride
    pieces = []
    for part in range(2):
        for lane in range(width // 128):
            pieces.append(held_ref[lane, pl.ds(mode * 2 + part, radial, stride=stride), :])
    values = jnp.concatenate(pieces, axis=1)
    values = dot3(split(forward_ref[0]), split(values))
    eigen = jnp.broadcast_to(radial_eigen_ref[0], (128, radial)).T[:, :1]
    denominator = 1.0 + diffusion_ref[field] * (eigen + axial_eigen_ref[...])
    inverse = 1.0 / denominator
    values = jnp.concatenate([values[:, :width] * inverse, values[:, width:] * inverse], axis=1)
    values = dot3(split(backward_ref[0]), split(values))
    values = jnp.concatenate([values[:, :width], values[:, width:]], axis=0)
    values = dot3(split(values), split(axial_ref[...]), ROWS_BY_ROWS)
    values = values.reshape(2, radial_devices, radial // radial_devices, width)
    first = place_ref[0] == 0
    out_ref[0, 0] = jnp.where(first, values[:, 0], values[:, 1])
    other = jnp.where(first, values[:, 1], values[:, 0]).reshape(radial, width)
    scale = code_scale(jnp.max(jnp.abs(other), axis=0, keepdims=True))
    send_ref[0, :radial, :] = linear_encode(other, scale).astype(BF16)
    send_ref[0, radial:, :] = jnp.broadcast_to(scale, (16, width)).astype(BF16)


def finish_body(place_ref, in_ref, _, __, out_ref):
    radial, width = out_ref.shape[2] * out_ref.shape[3], out_ref.shape[4]
    coded = in_ref[0].astype(F32)
    values = linear_decode(coded[:radial], coded[radial : radial + 1])
    out_ref[0, 0] = values.reshape(out_ref.shape[2:])


def params():
    return pltpu.CompilerParams(
        vmem_limit_bytes=VMEM_BYTES, dimension_semantics=("arbitrary",)
    )


def cost(microseconds):
    return pl.CostEstimate(
        flops=int(microseconds * 3e10), bytes_accessed=int(microseconds * 3e8), transcendentals=0
    )


def whole(shape):
    return pl.BlockSpec(shape, lambda *_: (0,) * len(shape))


SMEM = pl.BlockSpec(memory_space=pltpu.SMEM)
ANY = pl.BlockSpec(memory_space=pl.ANY)


def paired_plan(
    forcing,
    diffusion,
    axial_forward,
    axial_inverse_map,
    axial_eigenvalues,
    radial_forward,
    radial_backward,
    radial_eigenvalues,
):
    fields, slab, radial_block, width = forcing.shape
    processors, radial_devices = lax.axis_size("modes"), lax.axis_size("rad")
    devices = processors * radial_devices
    total, radial = slab * processors, radial_block * radial_devices
    own_modes = radial_forward.shape[0]
    retained = own_modes * devices
    near = processors // 2
    owners = near * radial_devices
    rows = radial_block // near
    group, kept, sent = 8, slab // 2, 96
    per_owner = 2 * own_modes
    side = lax.axis_index("modes") // near
    place = jnp.stack([lax.axis_index("rad"), side]).astype(jnp.int32)

    basis = window_basis(slab, total, 2 * retained - 1, kept - 1)
    spread = np.zeros((group, kept, slab, group))
    for row in range(group):
        spread[row, : kept - 1, :, row] = basis.T
    spread_upper, spread_lower = halves(spread.reshape(group * kept, slab * group))
    local, join_table = half_tables(total, retained, slab, basis, sent)
    local_upper, local_lower = halves(local)
    join_upper, join_lower = halves(join_table)
    axial_eigen = axial_eigenvalues.reshape(1, width)
    radial_eigen = radial_eigenvalues.reshape(own_modes, 1, radial)

    def of_side(table):
        return pl.BlockSpec((1,) + table.shape[1:], lambda i, p: (p[1], 0, 0))

    def encode(field, after):
        return pl.pallas_call(
            functools.partial(encode_body, group=group, kept=kept),
            grid=(near,),
            in_specs=[
                whole(spread_upper.shape),
                whole(spread_lower.shape),
                pl.BlockSpec((1, slab, rows, width), lambda i: (field, 0, i, 0)),
                ANY,
            ],
            out_specs=pl.BlockSpec((1, rows * kept, width), lambda i: (i, 0, 0)),
            out_shape=jax.ShapeDtypeStruct((near, rows * kept, width), BF16),
            compiler_params=params(),
            cost_estimate=cost(7),
            name="window_coefficients",
        )(jnp.asarray(spread_upper), jnp.asarray(spread_lower), forcing, after)

    def gather(received, after):
        step = 4
        return pl.pallas_call(
            functools.partial(gather_body, kept=kept, sent=sent, rows=step),
            grid_spec=pltpu.PrefetchScalarGridSpec(
                num_scalar_prefetch=1,
                grid=(rows // step,),
                in_specs=[
                    of_side(local_upper),
                    of_side(local_lower),
                    pl.BlockSpec((near, step * kept, width), lambda i, _: (0, i, 0)),
                    ANY,
                ],
                out_specs=[
                    pl.BlockSpec((step, retained, width), lambda i, _: (i, 0, 0)),
                    pl.BlockSpec((step * sent, width), lambda i, _: (i, 0)),
                ],
            ),
            out_shape=[
                jax.ShapeDtypeStruct((rows, retained, width), F32),
                jax.ShapeDtypeStruct((rows * sent, width), BF16),
            ],
            compiler_params=params(),
            cost_estimate=cost(5),
            name="half_sums",
        )(place, jnp.asarray(local_upper), jnp.asarray(local_lower), received, after)

    def join(own, received, after):
        step = 4
        block = rows * per_owner
        return pl.pallas_call(
            functools.partial(join_body, sent=sent, rows=step),
            grid_spec=pltpu.PrefetchScalarGridSpec(
                num_scalar_prefetch=1,
                grid=(rows // step,),
                in_specs=[
                    of_side(join_upper),
                    of_side(join_lower),
                    whole(axial_forward.shape),
                    pl.BlockSpec((step, retained, width), lambda i, _: (i, 0, 0)),
                    pl.BlockSpec((step * sent, width), lambda i, _: (i, 0)),
                    ANY,
                ],
                out_specs=whole((owners, block + 16, width)),
                scratch_shapes=[pltpu.VMEM((owners, block, width), F32)],
            ),
            out_shape=jax.ShapeDtypeStruct((owners, block + 16, width), BF16),
            compiler_params=params(),
            cost_estimate=cost(6),
            name="modal_axial_coefficients",
        )(place, jnp.asarray(join_upper), jnp.asarray(join_lower), axial_forward, own, received, after)

    out_shape = jax.ShapeDtypeStruct((fields, own_modes * radial_devices, 2, radial_block, width), F32)
    out_block = (1, 1, 2, radial_block, width)
    send_rows = radial + 16

    def solve(field, received, out, after):
        carried = [] if out is None else [out]
        first = 9
        return pl.pallas_call(
            functools.partial(solve_body, field=field, radial_devices=radial_devices),
            grid_spec=pltpu.PrefetchScalarGridSpec(
                num_scalar_prefetch=1,
                grid=(own_modes,),
                in_specs=[
                    SMEM,
                    whole(axial_eigen.shape),
                    pl.BlockSpec((1, 1, radial), lambda i, _: (i, 0, 0)),
                    whole(axial_inverse_map.shape),
                    pl.BlockSpec((1, radial, radial), lambda i, _: (i, 0, 0)),
                    pl.BlockSpec((1, radial, radial), lambda i, _: (i, 0, 0)),
                    whole(received.shape),
                ]
                + [ANY] * (1 + len(carried)),
                out_specs=[
                    pl.BlockSpec(out_block, lambda i, y: (field, y[0] * own_modes + i, 0, 0, 0)),
                    pl.BlockSpec((1, send_rows, width), lambda i, _: (i, 0, 0)),
                ],
                scratch_shapes=[
                    pltpu.VMEM((width // 128, radial * per_owner, 128), F32)
                ],
            ),
            out_shape=[out_shape, jax.ShapeDtypeStruct((own_modes, send_rows, width), BF16)],
            input_output_aliases={first: 0} if carried else {},
            compiler_params=params(),
            cost_estimate=cost(7),
            name="radial_solve",
        )(
            place,
            diffusion,
            axial_eigen,
            radial_eigen,
            axial_inverse_map,
            radial_forward,
            radial_backward,
            received,
            after,
            *carried,
        )

    def finish(field, received, out, after):
        return pl.pallas_call(
            finish_body,
            grid_spec=pltpu.PrefetchScalarGridSpec(
                num_scalar_prefetch=1,
                grid=(own_modes,),
                in_specs=[
                    pl.BlockSpec((1, send_rows, width), lambda i, _: (i, 0, 0)),
                    ANY,
                    ANY,
                ],
                out_specs=pl.BlockSpec(
                    out_block, lambda i, y: (field, (1 - y[0]) * own_modes + i, 0, 0, 0)
                ),
            ),
            out_shape=out_shape,
            input_output_aliases={2: 0},
            compiler_params=params(),
            cost_estimate=cost(2),
            name="partner_rows",
        )(place, received, out, after)

    sides = [list(range(near)), list(range(near, processors))]
    side_owners = [
        [m * radial_devices + y for m in members for y in range(radial_devices)] for members in sides
    ]

    def exchange(values, names, groups):
        return lax.all_to_all(
            values, names, split_axis=0, concat_axis=0, tiled=True, axis_index_groups=groups
        )

    def across(values):
        return lax.ppermute(values, "modes", [(i, (i + near) % processors) for i in range(processors)])

    def partner(values):
        return lax.ppermute(values, "rad", [(0, 1), (1, 0)])

    windows, own, away, spectra, partners = {}, {}, {}, {}, {}
    last, out = diffusion, None
    steps = (
        ["e0", "e1", "h0", "e2", "h1"]
        + ["j0", "h2", "j1", "s0", "j2"]
        + ["s1", "f0", "s2", "f1", "f2"]
    )
    for step in steps:
        field = int(step[1])
        if step[0] == "e":
            last = encode(field, last)
            windows[field] = exchange(last, "modes", sides)
        elif step[0] == "h":
            own[field], last = gather(windows[field], last)
            away[field] = across(last)
        elif step[0] == "j":
            last = join(own[field], away[field], last)
            spectra[field] = exchange(last, ("modes", "rad"), side_owners)
        elif step[0] == "s":
            out, last = solve(field, spectra[field], out, last)
            partners[field] = partner(last)
        else:
            out = finish(field, partners[field], out, last)
    return out


def azimuthal_tables(retained, points):
    row_index = jnp.arange(2 * retained, dtype=jnp.int32)
    wavenumber = row_index // 2
    quarter = (row_index % 2).astype(jnp.float32) * (0.5 * math.pi)
    theta_index = jnp.arange(points, dtype=jnp.int32)
    phase_index = wavenumber[:, None] * theta_index[None, :] % points
    radians = phase_index.astype(jnp.float32) * (2.0 * math.pi / points) + quarter[:, None]
    table = jnp.cos(radians) * (1.0 / math.sqrt(points))
    upper = table.astype(jnp.bfloat16)
    widened = lax.optimization_barrier(upper).astype(jnp.float32)
    lower = (table - widened).astype(jnp.bfloat16)
    return (upper, lower)


def modal_solve(spectral_coefficients, forward_map, backward, eigenvalues, axial_part, diffusion):
    highest_mode = lax.Precision.HIGHEST
    radial_coefficients = jnp.einsum(
        "hzv,bhtvp->bhtzp", forward_map, spectral_coefficients, precision=highest_mode
    )
    denominator = 1.0 + diffusion[:, None, None, None, None] * (
        eigenvalues[None, :, None, :, None] + axial_part[None, None, None, None, :]
    )
    return jnp.einsum(
        "mri,fmciq->fmcrq", backward, radial_coefficients / denominator, precision=highest_mode
    )


def general_plan(
    forcing,
    diffusion,
    axial_forward,
    axial_inverse_map,
    axial_eigenvalues,
    radial_forward,
    radial_backward,
    radial_eigenvalues,
):
    highest_mode = lax.Precision.HIGHEST
    fields, slab_points, radial_block, axial_points = forcing.shape
    mode_processors = lax.axis_size("modes")
    radial_devices = lax.axis_size("rad")
    total_theta = slab_points * mode_processors
    retained = radial_forward.shape[0] * mode_processors * radial_devices
    table_upper, table_lower = azimuthal_tables(retained, total_theta)
    flat_values = forcing.reshape(fields, slab_points, radial_block * axial_points)
    columns = lax.all_to_all(flat_values, "modes", split_axis=2, concat_axis=1, tiled=True)
    first = jnp.einsum("kt,ftc->fkc", table_upper, columns, preferred_element_type=jnp.float32)
    second = jnp.einsum("kt,ftc->fkc", table_lower, columns, preferred_element_type=jnp.float32)
    spectral = lax.all_to_all(first + second, "modes", split_axis=1, concat_axis=2, tiled=True)
    local_modes = spectral.shape[1] // 2
    spectral = spectral.reshape(fields, local_modes, 2, radial_block, axial_points)
    axial_coef = jnp.einsum("fmcrz,qz->fmcrq", spectral, axial_forward, precision=highest_mode)
    exchanged = lax.all_to_all(axial_coef, "rad", split_axis=4, concat_axis=3, tiled=True)
    forward_rows, backward_rows, eigen_rows = (
        lax.all_gather(radial_forward, "rad", axis=0, tiled=True),
        lax.all_gather(radial_backward, "rad", axis=0, tiled=True),
        lax.all_gather(radial_eigenvalues, "rad", axis=0, tiled=True),
    )
    axial_block = axial_points // radial_devices
    axial_part = lax.dynamic_slice_in_dim(
        axial_eigenvalues, lax.axis_index("rad") * axial_block, axial_block
    )
    solved = modal_solve(exchanged, forward_rows, backward_rows, eigen_rows, axial_part, diffusion)
    returned = lax.all_to_all(solved, "rad", split_axis=3, concat_axis=4, tiled=True)
    return jnp.einsum("fmcrq,zq->fmcrz", returned, axial_inverse_map, precision=highest_mode)


def per_device(forcing, diffusion, axial_forward, *maps):
    processors, radial_devices = lax.axis_size("modes"), lax.axis_size("rad")
    _, slab, radial_block, width = forcing.shape
    own_modes = maps[2].shape[0]
    paired = (
        radial_devices == 2
        and processors % 2 == 0
        and radial_block == 8 * processors
        and width % 128 == 0
        and own_modes == 4
        and slab % 32 == 0
        and slab * processors == 8 * own_modes * processors * radial_devices
    )
    plan = paired_plan if paired else general_plan
    return plan(forcing, diffusion, axial_forward, *maps)


def solution(mesh):
    in_specs = (
        P(None, "modes", "rad", None),
        P(),
        P(),
        P(),
        P(),
        P(("modes", "rad"), None, None),
        P(("modes", "rad"), None, None),
        P(("modes", "rad"), None),
    )
    out_specs = P(None, "modes", None, "rad", None)
    return jax.shard_map(
        per_device, mesh=mesh, in_specs=in_specs, out_specs=out_specs, check_vma=False
    )
```

```python
import functools
import math

import jax
import jax.numpy as jnp
import numpy as np
from jax import lax
from jax.experimental import pallas as pl
from jax.experimental.pallas import tpu as pltpu
from jax.sharding import PartitionSpec as P

BF16 = jnp.bfloat16
F32 = jnp.float32
VMEM_BYTES = 60 * 1024 * 1024

CODE_SPAN = 126.0
CODE_MID = 0.5
LN2 = math.log(2.0)
DECODE_SLOPE = 1.0 / (LN2 * CODE_SPAN)
DECODE_SHIFT = CODE_MID / CODE_SPAN
TINY = 1e-35


def code_scale(largest):
    return (largest * 1.008).astype(BF16).astype(F32)


def linear_encode(values, scale):
    inverse = jnp.where(scale > TINY, CODE_SPAN / jnp.maximum(scale, TINY), 0.0)
    return jnp.exp2(values * inverse + CODE_MID)


def linear_decode(coded, scale):
    return scale * (jnp.log(coded) * DECODE_SLOPE - DECODE_SHIFT)


def window_basis(window, total, band, rank):
    points = np.arange(window)
    inner = np.arange(1, window)
    diagonal = np.cos(np.pi * (2 * points - window + 1) / total) * np.cos(np.pi * band / total)
    beside = -np.sin(np.pi * inner / total) * np.sin(np.pi * (window - inner) / total)
    _, vectors = np.linalg.eigh(np.diag(diagonal) + np.diag(beside, 1) + np.diag(beside, -1))
    basis = vectors[:, :rank]
    signs = np.where(np.sum(basis * (points + 0.37)[:, None] ** 2, axis=0) < 0, -1.0, 1.0)
    return basis * signs


def waves(modes, points, total):
    return np.exp(-2j * np.pi * (modes[:, None] * points[None, :] % total) / total)


def interleave(values):
    return np.stack([values.real, values.imag], axis=1).reshape(-1, values.shape[-1])


def half_tables(total, retained, basis, sent):
    window = basis.shape[0]
    half, own = total // 2, retained // 2
    rank = basis.shape[1]
    envelope = window_basis(half, total, own, (sent - 1) // 2)
    local, join = [], []
    for side in range(2):
        points = side * half + np.arange(half)
        away = (1 - side) * own + np.arange(own)
        centre = (1 - side) * own + 0.5 * (own - 1)
        direct = waves(side * own + np.arange(own), points, total) / np.sqrt(total)
        carried = np.exp(-2j * np.pi * centre * points / total)[None, :] * envelope.T
        rows = np.concatenate([interleave(direct), interleave(carried)])
        rows = rows.reshape(rows.shape[0], -1, window) @ basis
        table = np.zeros((2 * own + sent, half // window, rank + 1))
        table[: rows.shape[0], :, :rank] = rows
        local.append(table)
        offsets = np.exp(-2j * np.pi * (away - centre)[:, None] * points[None, :] / total)
        weights = (offsets @ envelope) / np.sqrt(total)
        parts = np.zeros((own, 2, sent))
        count = 2 * weights.shape[1]
        parts[:, 0, 0:count:2], parts[:, 0, 1:count:2] = weights.real, -weights.imag
        parts[:, 1, 0:count:2], parts[:, 1, 1:count:2] = weights.imag, weights.real
        join.append(parts.reshape(2 * own, sent))
    return np.stack(local), np.stack(join[::-1])


def halves(table):
    upper = table.astype(np.float32).astype(jnp.bfloat16)
    lower = (table - upper.astype(np.float64)).astype(np.float32).astype(jnp.bfloat16)
    return upper, lower


def split(values):
    upper = values.astype(BF16)
    return upper, (values - upper.astype(F32)).astype(BF16)


def dot3(left, right, contract=((1,), (0,))):
    dims = (contract, ((), ()))
    dot = functools.partial(lax.dot_general, dimension_numbers=dims, preferred_element_type=F32)
    return dot(left[0], right[0]) + (dot(left[0], right[1]) + dot(left[1], right[0]))


ROWS_BY_ROWS = ((1,), (1,))


def encode_columns(values, kept):
    scale = code_scale(jnp.max(jnp.abs(values), axis=1, keepdims=True))
    place = lax.broadcasted_iota(jnp.int32, values.shape, 1)
    return jnp.where(place == kept - 1, scale, linear_encode(values, scale))


def decode_columns(coded, kept):
    values = linear_decode(coded, coded[:, kept - 1 : kept, :])
    place = lax.broadcasted_iota(jnp.int32, values.shape, 1)
    return jnp.where(place == kept - 1, 0.0, values)


def rows_body(_, forcing_ref, __, out_ref):
    out_ref[...] = forcing_ref[0]


def encode_body(
    _, own_upper, own_lower, other_upper, other_lower, own_ref, other_ref, __, *out_refs, group, kept
):
    step = pl.program_id(0)
    points, rows, width = other_ref.shape
    blocks = (own_ref[0].astype(F32), other_ref[...].astype(F32))
    tables = ((own_upper[0], own_lower[0]), (other_upper[0], other_lower[0]))
    parts = []
    for part in range(rows // group):
        sums = None
        for block, table in zip(blocks, tables):
            piece = block[:, part * group : (part + 1) * group, :].reshape(points * group, width)
            piece = piece.astype(BF16)
            for half in table:
                term = jnp.dot(half, piece, preferred_element_type=F32)
                sums = term if sums is None else sums + term
        coded = encode_columns(sums.reshape(group, kept, width), kept)
        parts.append(coded.reshape(group * kept, width).astype(BF16))
    coded = jnp.concatenate(parts, axis=0)
    for place, out_ref in enumerate(out_refs):

        @pl.when(step == place)
        def _(out_ref=out_ref):
            out_ref[...] = coded


def gather_body(_, upper_ref, lower_ref, *refs, kept, sent, rows):
    *in_refs, __, own_ref, send_ref = refs
    width = send_ref.shape[1]
    table = (upper_ref[0], lower_ref[0])
    own = own_ref.shape[1]
    for row in range(rows):
        coded = [ref[row * kept : (row + 1) * kept, :].astype(F32) for ref in in_refs]
        values = decode_columns(jnp.stack(coded), kept).reshape(len(in_refs) * kept, width)
        sums = dot3(table, split(values))
        own_ref[row] = sums[:own]
        send_ref[row * sent : (row + 1) * sent, :] = encode_columns(sums[None, own:], sent)[0].astype(BF16)


def join_body(
    _, upper_ref, lower_ref, axial_ref, own_ref, in_ref, __, out_ref, held_ref, *, sent, rows
):
    step = pl.program_id(0)
    width = in_ref.shape[1]
    owners, coded_rows = out_ref.shape[:2]
    block = coded_rows - 16
    table = (upper_ref[0], lower_ref[0])
    axial = split(axial_ref[...])
    for row in range(rows):
        coded = in_ref[row * sent : (row + 1) * sent, :].astype(F32)
        values = decode_columns(coded[None], sent)[0]
        spectrum = own_ref[row] + dot3(table, split(values))
        axial_coef = dot3(split(spectrum), axial, ROWS_BY_ROWS).reshape(owners, -1, width)
        each = axial_coef.shape[1]
        place = pl.multiple_of((step * rows + row) * each, each)
        held_ref[:, pl.ds(place, each), :] = axial_coef

    @pl.when(step == pl.num_programs(0) - 1)
    def _():
        for owner in range(owners):
            values = held_ref[owner]
            scale = code_scale(jnp.max(jnp.abs(values), axis=0, keepdims=True))
            out_ref[owner, :block, :] = linear_encode(values, scale).astype(BF16)
            out_ref[owner, block:, :] = jnp.broadcast_to(scale, (16, width)).astype(BF16)


def solve_body(
    place_ref,
    diffusion_ref,
    axial_eigen_ref,
    radial_eigen_ref,
    axial_ref,
    forward_ref,
    backward_ref,
    in_ref,
    *rest,
    field,
    radial_devices,
    modes,
):
    out_ref, send_ref, held_ref = rest[-3:]
    step = pl.program_id(0)
    each = forward_ref.shape[0]
    devices, coded_rows, width = in_ref.shape
    rows = coded_rows - 16
    chips = devices // radial_devices // 2
    stride = 2 * modes

    @pl.when(step == 0)
    def _():
        for source in range(devices):
            chip, core, block = source // radial_devices // 2, source // radial_devices % 2, source % radial_devices
            target = (block * 2 + core) * chips + chip
            coded = in_ref[source].astype(F32)
            values = linear_decode(coded[:rows], coded[rows : rows + 1])
            for lane in range(width // 128):
                held_ref[lane, target * rows : (target + 1) * rows, :] = values[
                    :, lane * 128 : (lane + 1) * 128
                ]

    radial = devices * rows // stride
    axial = split(axial_ref[...])
    first = place_ref[0] == 0
    for mode in range(each):
        pieces = []
        for part in range(2):
            for lane in range(width // 128):
                start = (step * each + mode) * 2 + part
                pieces.append(held_ref[lane, pl.ds(start, radial, stride=stride), :])
        values = jnp.concatenate(pieces, axis=1)
        values = dot3(split(forward_ref[mode]), split(values))
        eigen = jnp.broadcast_to(radial_eigen_ref[mode], (128, radial)).T[:, :1]
        denominator = 1.0 + diffusion_ref[field] * (eigen + axial_eigen_ref[...])
        inverse = 1.0 / denominator
        values = jnp.concatenate([values[:, :width] * inverse, values[:, width:] * inverse], axis=1)
        values = dot3(split(backward_ref[mode]), split(values))
        values = jnp.concatenate([values[:, :width], values[:, width:]], axis=0)
        values = dot3(split(values), axial, ROWS_BY_ROWS)
        values = values.reshape(2, radial_devices, radial // radial_devices, width)
        out_ref[0, mode] = jnp.where(first, values[:, 0], values[:, 1])
        other = jnp.where(first, values[:, 1], values[:, 0]).reshape(radial, width)
        scale = code_scale(jnp.max(jnp.abs(other), axis=0, keepdims=True))
        send_ref[mode, :radial, :] = linear_encode(other, scale).astype(BF16)
        send_ref[mode, radial:, :] = jnp.broadcast_to(scale, (16, width)).astype(BF16)


def finish_body(place_ref, in_ref, _, __, out_ref):
    radial = out_ref.shape[2] * out_ref.shape[3]
    for mode in range(in_ref.shape[0]):
        coded = in_ref[mode].astype(F32)
        values = linear_decode(coded[:radial], coded[radial : radial + 1])
        out_ref[0, mode] = values.reshape(out_ref.shape[2:])


def params():
    return pltpu.CompilerParams(
        vmem_limit_bytes=VMEM_BYTES, dimension_semantics=("arbitrary",)
    )


def cost(microseconds):
    return pl.CostEstimate(
        flops=int(microseconds * 3e10), bytes_accessed=int(microseconds * 3e8), transcendentals=0
    )


def whole(shape):
    return pl.BlockSpec(shape, lambda *_: (0,) * len(shape))


SMEM = pl.BlockSpec(memory_space=pltpu.SMEM)
ANY = pl.BlockSpec(memory_space=pl.ANY)


def paired_plan(
    forcing,
    diffusion,
    axial_forward,
    axial_inverse_map,
    axial_eigenvalues,
    radial_forward,
    radial_backward,
    radial_eigenvalues,
):
    fields, slab, radial_block, width = forcing.shape
    processors, radial_devices = lax.axis_size("modes"), lax.axis_size("rad")
    devices = processors * radial_devices
    total, radial = slab * processors, radial_block * radial_devices
    own_modes = radial_forward.shape[0]
    retained = own_modes * devices
    near = processors // 2
    owners = near * radial_devices
    rows = radial_block // near
    group, kept, sent = 8, slab * 3 // 4, 96
    per_owner = 2 * own_modes
    chips = near // 2
    position = lax.axis_index("modes")
    core, chip, side = position % 2, position // 2 % chips, position // near
    place = jnp.stack([lax.axis_index("rad"), side, core, chip, side * chips + chip]).astype(jnp.int32)

    window = 2 * slab
    basis = window_basis(window, total, 2 * retained - 1, kept - 1)
    spread = np.zeros((2, group, kept, slab, group))
    for row in range(group):
        spread[:, row, : kept - 1, :, row] = basis.reshape(2, slab, kept - 1).transpose(0, 2, 1)
    spread_upper, spread_lower = halves(spread.reshape(2, group * kept, slab * group))
    local, join_table = half_tables(total, retained, basis, sent)
    seen = [[here ^ step for step in range(chips)] for here in range(chips)]
    local = np.stack([table[:, order] for table in local for order in seen])
    local_upper, local_lower = halves(local.reshape(2 * chips, retained + sent, chips * kept))
    join_upper, join_lower = halves(join_table)
    axial_eigen = axial_eigenvalues.reshape(1, width)
    radial_eigen = radial_eigenvalues.reshape(own_modes, 1, radial)

    def chosen(table, index):
        return pl.BlockSpec((1,) + table.shape[1:], lambda i, p: (index(p), 0, 0))

    def encode(field, other, after):
        message = (rows * kept, width)
        return pl.pallas_call(
            functools.partial(encode_body, group=group, kept=kept),
            grid_spec=pltpu.PrefetchScalarGridSpec(
                num_scalar_prefetch=1,
                grid=(chips,),
                in_specs=[
                    chosen(spread_upper, lambda p: p[2]),
                    chosen(spread_lower, lambda p: p[2]),
                    chosen(spread_upper, lambda p: 1 - p[2]),
                    chosen(spread_lower, lambda p: 1 - p[2]),
                    pl.BlockSpec(
                        (1, slab, rows, width), lambda i, p: (field, 0, p[2] * chips + (p[3] ^ i), 0)
                    ),
                    pl.BlockSpec((slab, rows, width), lambda i, p: (0, p[3] ^ i, 0)),
                    ANY,
                ],
                out_specs=[whole(message)] * chips,
            ),
            out_shape=[jax.ShapeDtypeStruct(message, BF16)] * chips,
            compiler_params=params(),
            cost_estimate=cost(7),
            name="window_coefficients",
        )(
            place,
            jnp.asarray(spread_upper),
            jnp.asarray(spread_lower),
            jnp.asarray(spread_upper),
            jnp.asarray(spread_lower),
            forcing,
            other,
            after,
        )

    def gather(received, after):
        step = 4
        return pl.pallas_call(
            functools.partial(gather_body, kept=kept, sent=sent, rows=step),
            grid_spec=pltpu.PrefetchScalarGridSpec(
                num_scalar_prefetch=1,
                grid=(rows // step,),
                in_specs=[chosen(local_upper, lambda p: p[4]), chosen(local_lower, lambda p: p[4])]
                + [pl.BlockSpec((step * kept, width), lambda i, _: (i, 0))] * chips
                + [ANY],
                out_specs=[
                    pl.BlockSpec((step, retained, width), lambda i, _: (i, 0, 0)),
                    pl.BlockSpec((step * sent, width), lambda i, _: (i, 0)),
                ],
            ),
            out_shape=[
                jax.ShapeDtypeStruct((rows, retained, width), F32),
                jax.ShapeDtypeStruct((rows * sent, width), BF16),
            ],
            compiler_params=params(),
            cost_estimate=cost(5),
            name="half_sums",
        )(place, jnp.asarray(local_upper), jnp.asarray(local_lower), *received, after)

    def join(own, received, after):
        step = 4
        block = rows * per_owner
        return pl.pallas_call(
            functools.partial(join_body, sent=sent, rows=step),
            grid_spec=pltpu.PrefetchScalarGridSpec(
                num_scalar_prefetch=1,
                grid=(rows // step,),
                in_specs=[
                    chosen(join_upper, lambda p: p[1]),
                    chosen(join_lower, lambda p: p[1]),
                    whole(axial_forward.shape),
                    pl.BlockSpec((step, retained, width), lambda i, _: (i, 0, 0)),
                    pl.BlockSpec((step * sent, width), lambda i, _: (i, 0)),
                    ANY,
                ],
                out_specs=whole((owners, block + 16, width)),
                scratch_shapes=[pltpu.VMEM((owners, block, width), F32)],
            ),
            out_shape=jax.ShapeDtypeStruct((owners, block + 16, width), BF16),
            compiler_params=params(),
            cost_estimate=cost(6),
            name="modal_axial_coefficients",
        )(place, jnp.asarray(join_upper), jnp.asarray(join_lower), axial_forward, own, received, after)

    out_shape = jax.ShapeDtypeStruct((fields, own_modes * radial_devices, 2, radial_block, width), F32)
    each = 2
    turns = own_modes // each
    out_block = (1, each, 2, radial_block, width)
    send_rows = radial + 16

    def solve(field, received, out, after):
        carried = [] if out is None else [out]
        first = 9
        return pl.pallas_call(
            functools.partial(
                solve_body, field=field, radial_devices=radial_devices, modes=own_modes
            ),
            grid_spec=pltpu.PrefetchScalarGridSpec(
                num_scalar_prefetch=1,
                grid=(turns,),
                in_specs=[
                    SMEM,
                    whole(axial_eigen.shape),
                    pl.BlockSpec((each, 1, radial), lambda i, _: (i, 0, 0)),
                    whole(axial_inverse_map.shape),
                    pl.BlockSpec((each, radial, radial), lambda i, _: (i, 0, 0)),
                    pl.BlockSpec((each, radial, radial), lambda i, _: (i, 0, 0)),
                    whole(received.shape),
                ]
                + [ANY] * (1 + len(carried)),
                out_specs=[
                    pl.BlockSpec(out_block, lambda i, y: (field, y[0] * turns + i, 0, 0, 0)),
                    pl.BlockSpec((each, send_rows, width), lambda i, _: (i, 0, 0)),
                ],
                scratch_shapes=[
                    pltpu.VMEM((width // 128, radial * per_owner, 128), F32)
                ],
            ),
            out_shape=[out_shape, jax.ShapeDtypeStruct((own_modes, send_rows, width), BF16)],
            input_output_aliases={first: 0} if carried else {},
            compiler_params=params(),
            cost_estimate=cost(7),
            name="radial_solve",
        )(
            place,
            diffusion,
            axial_eigen,
            radial_eigen,
            axial_inverse_map,
            radial_forward,
            radial_backward,
            received,
            after,
            *carried,
        )

    def finish(field, received, out, after):
        return pl.pallas_call(
            finish_body,
            grid_spec=pltpu.PrefetchScalarGridSpec(
                num_scalar_prefetch=1,
                grid=(turns,),
                in_specs=[
                    pl.BlockSpec((each, send_rows, width), lambda i, _: (i, 0, 0)),
                    ANY,
                    ANY,
                ],
                out_specs=pl.BlockSpec(
                    out_block, lambda i, y: (field, (1 - y[0]) * turns + i, 0, 0, 0)
                ),
            ),
            out_shape=out_shape,
            input_output_aliases={2: 0},
            compiler_params=params(),
            cost_estimate=cost(2),
            name="partner_rows",
        )(place, received, out, after)

    side_owners = [list(range(owners)), list(range(owners, 2 * owners))]

    def exchange(values, names, groups):
        return lax.all_to_all(
            values, names, split_axis=0, concat_axis=0, tiled=True, axis_index_groups=groups
        )

    def flip(values, bits):
        return lax.ppermute(values, "modes", [(i, i ^ bits) for i in range(processors)])

    def other_rows(field, after):
        shape = (slab, radial_block // 2, width)
        return pl.pallas_call(
            rows_body,
            grid_spec=pltpu.PrefetchScalarGridSpec(
                num_scalar_prefetch=1,
                grid=(4,),
                in_specs=[
                    pl.BlockSpec(
                        (1, slab // 4) + shape[1:], lambda i, p: (field, i, 1 - p[2], 0)
                    ),
                    ANY,
                ],
                out_specs=pl.BlockSpec((slab // 4,) + shape[1:], lambda i, _: (i, 0, 0)),
            ),
            out_shape=jax.ShapeDtypeStruct(shape, BF16),
            compiler_params=params(),
            cost_estimate=cost(2),
            name="other_core_rows",
        )(place, forcing, after)

    def partner(values):
        return lax.ppermute(values, "rad", [(0, 1), (1, 0)])

    windows, own, away, spectra, partners = {}, {}, {}, {}, {}
    swapped = {}
    last, out = diffusion, None
    steps = (
        ["c0", "c1", "e0", "c2", "e1", "h0", "e2", "h1"]
        + ["j0", "h2", "j1", "s0", "j2"]
        + ["s1", "f0", "s2", "f1", "f2"]
    )
    for step in steps:
        field = int(step[1])
        if step[0] == "c":
            last = other_rows(field, last)
            swapped[field] = flip(last, 1)
        elif step[0] == "e":
            made = encode(field, swapped[field], last)
            last = made[0]
            windows[field] = [last] + [flip(made[j], 2 * j) for j in range(1, chips)]
        elif step[0] == "h":
            own[field], last = gather(windows[field], last)
            away[field] = flip(last, near)
        elif step[0] == "j":
            last = join(own[field], away[field], last)
            spectra[field] = exchange(last, ("modes", "rad"), side_owners)
        elif step[0] == "s":
            out, last = solve(field, spectra[field], out, last)
            partners[field] = partner(last)
        else:
            out = finish(field, partners[field], out, last)
    return out


def azimuthal_tables(retained, points):
    row_index = jnp.arange(2 * retained, dtype=jnp.int32)
    wavenumber = row_index // 2
    quarter = (row_index % 2).astype(jnp.float32) * (0.5 * math.pi)
    theta_index = jnp.arange(points, dtype=jnp.int32)
    phase_index = wavenumber[:, None] * theta_index[None, :] % points
    radians = phase_index.astype(jnp.float32) * (2.0 * math.pi / points) + quarter[:, None]
    table = jnp.cos(radians) * (1.0 / math.sqrt(points))
    upper = table.astype(jnp.bfloat16)
    widened = lax.optimization_barrier(upper).astype(jnp.float32)
    lower = (table - widened).astype(jnp.bfloat16)
    return (upper, lower)


def modal_solve(spectral_coefficients, forward_map, backward, eigenvalues, axial_part, diffusion):
    highest_mode = lax.Precision.HIGHEST
    radial_coefficients = jnp.einsum(
        "hzv,bhtvp->bhtzp", forward_map, spectral_coefficients, precision=highest_mode
    )
    denominator = 1.0 + diffusion[:, None, None, None, None] * (
        eigenvalues[None, :, None, :, None] + axial_part[None, None, None, None, :]
    )
    return jnp.einsum(
        "mri,fmciq->fmcrq", backward, radial_coefficients / denominator, precision=highest_mode
    )


def general_plan(
    forcing,
    diffusion,
    axial_forward,
    axial_inverse_map,
    axial_eigenvalues,
    radial_forward,
    radial_backward,
    radial_eigenvalues,
):
    highest_mode = lax.Precision.HIGHEST
    fields, slab_points, radial_block, axial_points = forcing.shape
    mode_processors = lax.axis_size("modes")
    radial_devices = lax.axis_size("rad")
    total_theta = slab_points * mode_processors
    retained = radial_forward.shape[0] * mode_processors * radial_devices
    table_upper, table_lower = azimuthal_tables(retained, total_theta)
    flat_values = forcing.reshape(fields, slab_points, radial_block * axial_points)
    columns = lax.all_to_all(flat_values, "modes", split_axis=2, concat_axis=1, tiled=True)
    first = jnp.einsum("kt,ftc->fkc", table_upper, columns, preferred_element_type=jnp.float32)
    second = jnp.einsum("kt,ftc->fkc", table_lower, columns, preferred_element_type=jnp.float32)
    spectral = lax.all_to_all(first + second, "modes", split_axis=1, concat_axis=2, tiled=True)
    local_modes = spectral.shape[1] // 2
    spectral = spectral.reshape(fields, local_modes, 2, radial_block, axial_points)
    axial_coef = jnp.einsum("fmcrz,qz->fmcrq", spectral, axial_forward, precision=highest_mode)
    exchanged = lax.all_to_all(axial_coef, "rad", split_axis=4, concat_axis=3, tiled=True)
    forward_rows, backward_rows, eigen_rows = (
        lax.all_gather(radial_forward, "rad", axis=0, tiled=True),
        lax.all_gather(radial_backward, "rad", axis=0, tiled=True),
        lax.all_gather(radial_eigenvalues, "rad", axis=0, tiled=True),
    )
    axial_block = axial_points // radial_devices
    axial_part = lax.dynamic_slice_in_dim(
        axial_eigenvalues, lax.axis_index("rad") * axial_block, axial_block
    )
    solved = modal_solve(exchanged, forward_rows, backward_rows, eigen_rows, axial_part, diffusion)
    returned = lax.all_to_all(solved, "rad", split_axis=3, concat_axis=4, tiled=True)
    return jnp.einsum("fmcrq,zq->fmcrz", returned, axial_inverse_map, precision=highest_mode)


def per_device(forcing, diffusion, axial_forward, *maps):
    processors, radial_devices = lax.axis_size("modes"), lax.axis_size("rad")
    _, slab, radial_block, width = forcing.shape
    own_modes = maps[2].shape[0]
    paired = (
        radial_devices == 2
        and processors >= 8
        and processors & (processors - 1) == 0
        and radial_block == 8 * processors
        and width % 128 == 0
        and own_modes == 4
        and slab % 32 == 0
        and slab * processors == 8 * own_modes * processors * radial_devices
    )
    plan = paired_plan if paired else general_plan
    return plan(forcing, diffusion, axial_forward, *maps)


def solution(mesh):
    in_specs = (
        P(None, "modes", "rad", None),
        P(),
        P(),
        P(),
        P(),
        P(("modes", "rad"), None, None),
        P(("modes", "rad"), None, None),
        P(("modes", "rad"), None),
    )
    out_specs = P(None, "modes", None, "rad", None)
    return jax.shard_map(
        per_device, mesh=mesh, in_specs=in_specs, out_specs=out_specs, check_vma=False
    )
```

```python
import functools
import math

import jax
import jax.numpy as jnp
import numpy as np
from jax import lax
from jax.experimental import pallas as pl
from jax.experimental.pallas import tpu as pltpu
from jax.sharding import PartitionSpec as P

BF16 = jnp.bfloat16
F32 = jnp.float32
VMEM_BYTES = 40 * 1024 * 1024

CODE_SPAN = 126.0
CODE_MID = 0.5
LN2 = math.log(2.0)
DECODE_SLOPE = 1.0 / (LN2 * CODE_SPAN)
DECODE_SHIFT = CODE_MID / CODE_SPAN
TINY = 1e-35


def code_scale(largest):
    return (largest * 1.008).astype(BF16).astype(F32)


def linear_encode(values, scale):
    inverse = jnp.where(scale > TINY, CODE_SPAN / jnp.maximum(scale, TINY), 0.0)
    return jnp.exp2(values * inverse + CODE_MID)


def linear_decode(coded, scale):
    return scale * (jnp.log(coded) * DECODE_SLOPE - DECODE_SHIFT)


def window_basis(window, total, band, rank):
    points = np.arange(window)
    inner = np.arange(1, window)
    diagonal = np.cos(np.pi * (2 * points - window + 1) / total) * np.cos(np.pi * band / total)
    beside = -np.sin(np.pi * inner / total) * np.sin(np.pi * (window - inner) / total)
    _, vectors = np.linalg.eigh(np.diag(diagonal) + np.diag(beside, 1) + np.diag(beside, -1))
    basis = vectors[:, :rank]
    signs = np.where(np.sum(basis * (points + 0.37)[:, None] ** 2, axis=0) < 0, -1.0, 1.0)
    return basis * signs


def waves(modes, points, total):
    return np.exp(-2j * np.pi * (modes[:, None] * points[None, :] % total) / total)


def interleave(values):
    return np.stack([values.real, values.imag], axis=1).reshape(-1, values.shape[-1])


def half_tables(total, retained, basis, sent):
    window = basis.shape[0]
    half, own = total // 2, retained // 2
    rank = basis.shape[1]
    envelope = window_basis(half, total, own, sent // 2)
    local, join = [], []
    for side in range(2):
        points = side * half + np.arange(half)
        away = (1 - side) * own + np.arange(own)
        centre = (1 - side) * own + 0.5 * (own - 1)
        direct = waves(side * own + np.arange(own), points, total) / np.sqrt(total)
        carried = np.exp(-2j * np.pi * centre * points / total)[None, :] * envelope.T
        rows = np.concatenate([interleave(direct), interleave(carried)])
        rows = rows.reshape(rows.shape[0], -1, window) @ basis
        table = np.zeros((2 * own + sent, half // window, rank + 1))
        table[: rows.shape[0], :, :rank] = rows
        local.append(table)
        offsets = np.exp(-2j * np.pi * (away - centre)[:, None] * points[None, :] / total)
        weights = (offsets @ envelope) / np.sqrt(total)
        parts = np.zeros((own, 2, sent))
        count = 2 * weights.shape[1]
        parts[:, 0, 0:count:2], parts[:, 0, 1:count:2] = weights.real, -weights.imag
        parts[:, 1, 0:count:2], parts[:, 1, 1:count:2] = weights.imag, weights.real
        join.append(parts.reshape(2 * own, sent))
    return np.stack(local), np.stack(join[::-1])


def halves(table):
    upper = table.astype(np.float32).astype(jnp.bfloat16)
    lower = (table - upper.astype(np.float64)).astype(np.float32).astype(jnp.bfloat16)
    return upper, lower


def split(values):
    upper = values.astype(BF16)
    return upper, (values - upper.astype(F32)).astype(BF16)


def dot3(left, right, contract=((1,), (0,))):
    dims = (contract, ((), ()))
    dot = functools.partial(lax.dot_general, dimension_numbers=dims, preferred_element_type=F32)
    return dot(left[0], right[0]) + (dot(left[0], right[1]) + dot(left[1], right[0]))


ROWS_BY_ROWS = ((1,), (1,))


def encode_columns(values, kept):
    scale = code_scale(jnp.max(jnp.abs(values), axis=1, keepdims=True))
    place = lax.broadcasted_iota(jnp.int32, values.shape, 1)
    return jnp.where(place == kept - 1, scale, linear_encode(values, scale))


def decode_columns(coded, kept):
    values = linear_decode(coded, coded[:, kept - 1 : kept, :])
    place = lax.broadcasted_iota(jnp.int32, values.shape, 1)
    return jnp.where(place == kept - 1, 0.0, values)


def rows_body(_, forcing_ref, __, out_ref):
    out_ref[...] = forcing_ref[0]


def encode_body(
    _, own_upper, own_lower, other_upper, other_lower, own_ref, other_ref, __, *out_refs, group, kept, parts
):
    step = pl.program_id(0)
    points, _, width = other_ref.shape
    blocks = (own_ref[0].astype(F32), other_ref[...].astype(F32))
    tables = ((own_upper[0], own_lower[0]), (other_upper[0], other_lower[0]))
    made = []
    for part in parts:
        sums = None
        for block, table in zip(blocks, tables):
            piece = block[:, part * group : (part + 1) * group, :].reshape(points * group, width)
            piece = piece.astype(BF16)
            for half in table:
                term = jnp.dot(half, piece, preferred_element_type=F32)
                sums = term if sums is None else sums + term
        coded = encode_columns(sums.reshape(group, kept, width), kept)
        made.append(coded.reshape(group * kept, width).astype(BF16))
    coded = jnp.concatenate(made, axis=0)
    for place, out_ref in enumerate(out_refs):

        @pl.when(step == place)
        def _(out_ref=out_ref):
            out_ref[...] = coded


def gather_body(_, upper_ref, lower_ref, *refs, kept, rows):
    *in_refs, __, own_ref, send_ref, scale_ref = refs
    step = pl.program_id(0)
    width = send_ref.shape[1]
    table = (upper_ref[0], lower_ref[0])
    own = own_ref.shape[1]
    made = []
    for row in range(rows):
        here = slice(row * kept, (row + 1) * kept)
        coded = jnp.stack([ref[here, :].astype(F32) for ref in in_refs])
        sums = dot3(table, split(decode_columns(coded, kept).reshape(-1, width)))
        own_ref[row] = sums[:own]
        scale = code_scale(jnp.max(jnp.abs(sums[own:]), axis=0, keepdims=True))
        scale_ref[pl.ds(step * rows + row, 1), :] = scale
        made.append(linear_encode(sums[own:], scale))
    made = jnp.concatenate(made, axis=0).astype(BF16)
    count = made.shape[0]
    send_ref[pl.ds(pl.multiple_of(step * count, count), count), :] = made

    @pl.when(step == pl.num_programs(0) - 1)
    def _():
        send_ref[send_ref.shape[0] - scale_ref.shape[0] :, :] = scale_ref[...].astype(BF16)


def join_body(_, upper_ref, lower_ref, axial_ref, *refs, sent, rows, turns):
    *pieces, __, out_ref, held_ref = refs
    step = pl.program_id(0)
    owners, coded_rows, width = out_ref.shape
    block = coded_rows - 16
    table = (upper_ref[0], lower_ref[0])
    axial = split(axial_ref[...])

    def add(own_ref, in_ref, start):
        total = in_ref.shape[0] // (sent + 1)
        count = rows * sent
        local = step - start
        coded = in_ref[pl.ds(pl.multiple_of(local * count, count), count), :].astype(F32)
        scales = in_ref[total * sent :, :].astype(F32)
        place = lax.broadcasted_iota(jnp.int32, scales.shape, 0)
        for row in range(rows):
            here = place == local * rows + row
            scale = jnp.sum(jnp.where(here, scales, 0.0), axis=0, keepdims=True)
            values = linear_decode(coded[row * sent : (row + 1) * sent], scale)
            spectrum = own_ref[row] + dot3(table, split(values))
            axial_coef = dot3(split(spectrum), axial, ROWS_BY_ROWS).reshape(owners, -1, width)
            each = axial_coef.shape[1]
            target = pl.multiple_of((step * rows + row) * each, each)
            held_ref[:, pl.ds(target, each), :] = axial_coef

    if len(turns) == 1:
        add(*pieces, 0)
    else:
        for number, (start, count) in enumerate(turns):
            here = pieces[2 * number : 2 * number + 2]
            pl.when((step >= start) & (step < start + count))(functools.partial(add, *here, start))

    @pl.when(step == pl.num_programs(0) - 1)
    def _():
        for owner in range(owners):
            values = held_ref[owner]
            scale = code_scale(jnp.max(jnp.abs(values), axis=0, keepdims=True))
            out_ref[owner, :block, :] = linear_encode(values, scale).astype(BF16)
            out_ref[owner, block:, :] = jnp.broadcast_to(scale, (16, width)).astype(BF16)


def solve_body(
    place_ref,
    diffusion_ref,
    axial_eigen_ref,
    radial_eigen_ref,
    axial_ref,
    forward_ref,
    backward_ref,
    *rest,
    field,
    radial_devices,
    modes,
    first_mode,
    pieces,
):
    in_refs = rest[:pieces]
    out_ref, send_ref, held_ref = rest[-3:]
    step = pl.program_id(0)
    each = forward_ref.shape[0]
    devices, _, width = in_refs[0].shape
    rows = sum(ref.shape[1] - 16 for ref in in_refs)
    chips = devices // radial_devices // 2
    stride = 2 * modes

    @pl.when(step == 0)
    def _():
        for source in range(devices):
            chip, core, block = source // radial_devices // 2, source // radial_devices % 2, source % radial_devices
            target = (block * 2 + core) * chips + chip
            start = target * rows
            for in_ref in in_refs:
                count = in_ref.shape[1] - 16
                coded = in_ref[source].astype(F32)
                values = linear_decode(coded[:count], coded[count : count + 1])
                for lane in range(width // 128):
                    held_ref[lane, start : start + count, :] = values[:, lane * 128 : (lane + 1) * 128]
                start += count

    radial = devices * rows // stride
    axial = split(axial_ref[...])
    first = place_ref[0] == 0
    for mode in range(each):
        columns = []
        for part in range(2):
            for lane in range(width // 128):
                start = (first_mode + step * each + mode) * 2 + part
                columns.append(held_ref[lane, pl.ds(start, radial, stride=stride), :])
        values = jnp.concatenate(columns, axis=1)
        values = dot3(split(forward_ref[mode]), split(values))
        eigen = jnp.broadcast_to(radial_eigen_ref[mode], (128, radial)).T[:, :1]
        denominator = 1.0 + diffusion_ref[field] * (eigen + axial_eigen_ref[...])
        inverse = 1.0 / denominator
        values = jnp.concatenate([values[:, :width] * inverse, values[:, width:] * inverse], axis=1)
        values = dot3(split(backward_ref[mode]), split(values))
        values = jnp.concatenate([values[:, :width], values[:, width:]], axis=0)
        values = dot3(split(values), axial, ROWS_BY_ROWS)
        values = values.reshape(2, radial_devices, radial // radial_devices, width)
        out_ref[0, mode] = jnp.where(first, values[:, 0], values[:, 1])
        other = jnp.where(first, values[:, 1], values[:, 0]).reshape(radial, width)
        scale = code_scale(jnp.max(jnp.abs(other), axis=0, keepdims=True))
        send_ref[mode, :radial, :] = linear_encode(other, scale).astype(BF16)
        send_ref[mode, radial:, :] = jnp.broadcast_to(scale, (16, width)).astype(BF16)


def finish_body(place_ref, in_ref, _, __, out_ref):
    radial = out_ref.shape[2] * out_ref.shape[3]
    for mode in range(in_ref.shape[0]):
        coded = in_ref[mode].astype(F32)
        values = linear_decode(coded[:radial], coded[radial : radial + 1])
        out_ref[0, mode] = values.reshape(out_ref.shape[2:])


def params():
    return pltpu.CompilerParams(
        vmem_limit_bytes=VMEM_BYTES, dimension_semantics=("arbitrary",)
    )


def cost(microseconds):
    return pl.CostEstimate(
        flops=int(microseconds * 3e10), bytes_accessed=int(microseconds * 3e8), transcendentals=0
    )


def whole(shape):
    return pl.BlockSpec(shape, lambda *_: (0,) * len(shape))


SMEM = pl.BlockSpec(memory_space=pltpu.SMEM)
ANY = pl.BlockSpec(memory_space=pl.ANY)


def paired_plan(
    forcing,
    diffusion,
    axial_forward,
    axial_inverse_map,
    axial_eigenvalues,
    radial_forward,
    radial_backward,
    radial_eigenvalues,
):
    fields, slab, radial_block, width = forcing.shape
    processors, radial_devices = lax.axis_size("modes"), lax.axis_size("rad")
    devices = processors * radial_devices
    total, radial = slab * processors, radial_block * radial_devices
    own_modes = radial_forward.shape[0]
    retained = own_modes * devices
    near = processors // 2
    owners = near * radial_devices
    rows = radial_block // near
    group, kept, sent = 8, slab * 3 // 4, 88
    per_owner = 2 * own_modes
    chips = near // 2
    position = lax.axis_index("modes")
    core, chip, side = position % 2, position // 2 % chips, position // near
    place = jnp.stack([lax.axis_index("rad"), side, core, chip, side * chips + chip]).astype(jnp.int32)

    window = 2 * slab
    basis = window_basis(window, total, 2 * retained - 1, kept - 1)
    spread = np.zeros((2, group, kept, slab, group))
    for row in range(group):
        spread[:, row, : kept - 1, :, row] = basis.reshape(2, slab, kept - 1).transpose(0, 2, 1)
    spread_upper, spread_lower = halves(spread.reshape(2, group * kept, slab * group))
    local, join_table = half_tables(total, retained, basis, sent)
    seen = [[here ^ step for step in range(chips)] for here in range(chips)]
    local = np.stack([table[:, order] for table in local for order in seen])
    local_upper, local_lower = halves(local.reshape(2 * chips, retained + sent, chips * kept))
    join_upper, join_lower = halves(join_table)
    axial_eigen = axial_eigenvalues.reshape(1, width)
    radial_eigen = radial_eigenvalues.reshape(own_modes, 1, radial)

    def chosen(table, index):
        return pl.BlockSpec((1,) + table.shape[1:], lambda i, p: (index(p), 0, 0))

    def encode(field, parts, other, after):
        message = (len(parts) * group * kept, width)
        return pl.pallas_call(
            functools.partial(encode_body, group=group, kept=kept, parts=parts),
            grid_spec=pltpu.PrefetchScalarGridSpec(
                num_scalar_prefetch=1,
                grid=(chips,),
                in_specs=[
                    chosen(spread_upper, lambda p: p[2]),
                    chosen(spread_lower, lambda p: p[2]),
                    chosen(spread_upper, lambda p: 1 - p[2]),
                    chosen(spread_lower, lambda p: 1 - p[2]),
                    pl.BlockSpec(
                        (1, slab, rows, width), lambda i, p: (field, 0, p[2] * chips + (p[3] ^ i), 0)
                    ),
                    pl.BlockSpec((slab, rows, width), lambda i, p: (0, (p[3] ^ i), 0)),
                    ANY,
                ],
                out_specs=[whole(message)] * chips,
            ),
            out_shape=[jax.ShapeDtypeStruct(message, BF16)] * chips,
            compiler_params=params(),
            cost_estimate=cost(7),
            name="window_coefficients",
        )(
            place,
            jnp.asarray(spread_upper),
            jnp.asarray(spread_lower),
            jnp.asarray(spread_upper),
            jnp.asarray(spread_lower),
            forcing,
            other,
            after,
        )

    def gather(received, after):
        step = 4
        rows = received[0].shape[0] // kept
        message = (rows * (sent + 1), width)
        return pl.pallas_call(
            functools.partial(gather_body, kept=kept, rows=step),
            grid_spec=pltpu.PrefetchScalarGridSpec(
                num_scalar_prefetch=1,
                grid=(rows // step,),
                in_specs=[chosen(local_upper, lambda p: p[4]), chosen(local_lower, lambda p: p[4])]
                + [pl.BlockSpec((step * kept, width), lambda i, _: (i, 0))] * chips
                + [ANY],
                out_specs=[
                    pl.BlockSpec((step, retained, width), lambda i, _: (i, 0, 0)),
                    whole(message),
                ],
                scratch_shapes=[pltpu.VMEM((rows, width), F32)],
            ),
            out_shape=[
                jax.ShapeDtypeStruct((rows, retained, width), F32),
                jax.ShapeDtypeStruct(message, BF16),
            ],
            compiler_params=params(),
            cost_estimate=cost(5),
            name="half_sums",
        )(place, jnp.asarray(local_upper), jnp.asarray(local_lower), *received, after)

    def join(pieces, after):
        step = 4
        turns, specs, start = [], [], 0
        for own, message in pieces:
            count = own.shape[0] // step

            def turn(i, start=start, count=count):
                return jnp.clip(i - start, 0, count - 1)

            specs.append(pl.BlockSpec((step, retained, width), lambda i, _, turn=turn: (turn(i), 0, 0)))
            specs.append(whole(message.shape))
            turns.append((start, count))
            start += count
        block = start * step * per_owner
        return pl.pallas_call(
            functools.partial(join_body, sent=sent, rows=step, turns=turns),
            grid_spec=pltpu.PrefetchScalarGridSpec(
                num_scalar_prefetch=1,
                grid=(start,),
                in_specs=[
                    chosen(join_upper, lambda p: p[1]),
                    chosen(join_lower, lambda p: p[1]),
                    whole(axial_forward.shape),
                ]
                + specs
                + [ANY],
                out_specs=whole((owners, block + 16, width)),
                scratch_shapes=[pltpu.VMEM((owners, block, width), F32)],
            ),
            out_shape=jax.ShapeDtypeStruct((owners, block + 16, width), BF16),
            compiler_params=params(),
            cost_estimate=cost(6),
            name="modal_axial_coefficients",
        )(
            place,
            jnp.asarray(join_upper),
            jnp.asarray(join_lower),
            axial_forward,
            *[value for piece in pieces for value in piece],
            after,
        )

    out_shape = jax.ShapeDtypeStruct((fields, own_modes * radial_devices, 2, radial_block, width), F32)
    each = 2
    turns = own_modes // each
    out_block = (1, each, 2, radial_block, width)
    send_rows = radial + 16

    def solve(field, modes, received, out, after):
        carried = [] if out is None else [out]
        begin = modes[0] // each
        count = len(modes) // each
        return pl.pallas_call(
            functools.partial(
                solve_body,
                field=field,
                radial_devices=radial_devices,
                modes=own_modes,
                first_mode=modes[0],
                pieces=len(received),
            ),
            grid_spec=pltpu.PrefetchScalarGridSpec(
                num_scalar_prefetch=1,
                grid=(count,),
                in_specs=[
                    SMEM,
                    whole(axial_eigen.shape),
                    pl.BlockSpec((each, 1, radial), lambda i, _: (begin + i, 0, 0)),
                    whole(axial_inverse_map.shape),
                    pl.BlockSpec((each, radial, radial), lambda i, _: (begin + i, 0, 0)),
                    pl.BlockSpec((each, radial, radial), lambda i, _: (begin + i, 0, 0)),
                ]
                + [whole(piece.shape) for piece in received]
                + [ANY] * (1 + len(carried)),
                out_specs=[
                    pl.BlockSpec(out_block, lambda i, y: (field, y[0] * turns + begin + i, 0, 0, 0)),
                    pl.BlockSpec((each, send_rows, width), lambda i, _: (i, 0, 0)),
                ],
                scratch_shapes=[pltpu.VMEM((width // 128, radial * per_owner, 128), F32)],
            ),
            out_shape=[out_shape, jax.ShapeDtypeStruct((len(modes), send_rows, width), BF16)],
            input_output_aliases={8 + len(received): 0} if carried else {},
            compiler_params=params(),
            cost_estimate=cost(7),
            name="radial_solve",
        )(
            place,
            diffusion,
            axial_eigen,
            radial_eigen,
            axial_inverse_map,
            radial_forward,
            radial_backward,
            *received,
            after,
            *carried,
        )

    def finish(field, modes, received, out, after):
        begin = modes[0] // each
        return pl.pallas_call(
            finish_body,
            grid_spec=pltpu.PrefetchScalarGridSpec(
                num_scalar_prefetch=1,
                grid=(len(modes) // each,),
                in_specs=[
                    pl.BlockSpec((each, send_rows, width), lambda i, _: (i, 0, 0)),
                    ANY,
                    ANY,
                ],
                out_specs=pl.BlockSpec(
                    out_block, lambda i, y: (field, (1 - y[0]) * turns + begin + i, 0, 0, 0)
                ),
            ),
            out_shape=out_shape,
            input_output_aliases={2: 0},
            compiler_params=params(),
            cost_estimate=cost(2),
            name="partner_rows",
        )(place, received, out, after)

    side_owners = [list(range(owners)), list(range(owners, 2 * owners))]

    def exchange(values, names, groups):
        return lax.all_to_all(
            values, names, split_axis=0, concat_axis=0, tiled=True, axis_index_groups=groups
        )

    def flip(values, bits):
        return lax.ppermute(values, "modes", [(i, i ^ bits) for i in range(processors)])

    def other_rows(field, after):
        shape = (slab, radial_block // 2, width)
        return pl.pallas_call(
            rows_body,
            grid_spec=pltpu.PrefetchScalarGridSpec(
                num_scalar_prefetch=1,
                grid=(4,),
                in_specs=[
                    pl.BlockSpec(
                        (1, slab // 4) + shape[1:], lambda i, p: (field, i, 1 - p[2], 0)
                    ),
                    ANY,
                ],
                out_specs=pl.BlockSpec((slab // 4,) + shape[1:], lambda i, _: (i, 0, 0)),
            ),
            out_shape=jax.ShapeDtypeStruct(shape, BF16),
            compiler_params=params(),
            cost_estimate=cost(2),
            name="other_core_rows",
        )(place, forcing, after)

    def partner(values):
        return lax.ppermute(values, "rad", [(0, 1), (1, 0)])

    both = (0, 1)
    every = tuple(range(own_modes))
    head, tail = every[: own_modes // 2], every[own_modes // 2 :]
    steps = [
        ("rows", 0, both),
        ("rows", 1, both),
        ("encode", 0, both),
        ("rows", 2, both),
        ("encode", 1, both),
        ("gather", 0, both),
        ("encode", 2, both),
        ("gather", 1, both),
        ("join", 0, (both,)),
        ("gather", 2, both),
        ("join", 1, (both,)),
        ("solve", 0, every),
        ("join", 2, (both,)),
        ("solve", 1, every),
        ("finish", 0, every),
        ("solve", 2, head),
        ("solve", 2, tail),
        ("finish", 1, every),
        ("finish", 2, head),
        ("finish", 2, tail),
    ]
    swapped, windows, own, away, partners = {}, {}, {}, {}, {}
    spectra = {field: [] for field in range(fields)}
    last, out = diffusion, None
    for name, field, which in steps:
        key = (field, which)
        if name == "rows":
            last = other_rows(field, last)
            swapped[field] = flip(last, 1)
        elif name == "encode":
            made = encode(field, which, swapped[field], last)
            last = made[0]
            windows[key] = [last] + [flip(made[j], 2 * j) for j in range(1, chips)]
        elif name == "gather":
            own[key], last = gather(windows[key], last)
            away[key] = flip(last, near)
        elif name == "join":
            last = join([(own[field, part], away[field, part]) for part in which], last)
            spectra[field].append(exchange(last, ("modes", "rad"), side_owners))
        elif name == "solve":
            out, last = solve(field, which, spectra[field], out, last)
            partners[key] = partner(last)
        else:
            out = finish(field, which, partners[key], out, last)
    return out


def azimuthal_tables(retained, points):
    row_index = jnp.arange(2 * retained, dtype=jnp.int32)
    wavenumber = row_index // 2
    quarter = (row_index % 2).astype(jnp.float32) * (0.5 * math.pi)
    theta_index = jnp.arange(points, dtype=jnp.int32)
    phase_index = wavenumber[:, None] * theta_index[None, :] % points
    radians = phase_index.astype(jnp.float32) * (2.0 * math.pi / points) + quarter[:, None]
    table = jnp.cos(radians) * (1.0 / math.sqrt(points))
    upper = table.astype(jnp.bfloat16)
    widened = lax.optimization_barrier(upper).astype(jnp.float32)
    lower = (table - widened).astype(jnp.bfloat16)
    return (upper, lower)


def modal_solve(spectral_coefficients, forward_map, backward, eigenvalues, axial_part, diffusion):
    highest_mode = lax.Precision.HIGHEST
    radial_coefficients = jnp.einsum(
        "hzv,bhtvp->bhtzp", forward_map, spectral_coefficients, precision=highest_mode
    )
    denominator = 1.0 + diffusion[:, None, None, None, None] * (
        eigenvalues[None, :, None, :, None] + axial_part[None, None, None, None, :]
    )
    return jnp.einsum(
        "mri,fmciq->fmcrq", backward, radial_coefficients / denominator, precision=highest_mode
    )


def general_plan(
    forcing,
    diffusion,
    axial_forward,
    axial_inverse_map,
    axial_eigenvalues,
    radial_forward,
    radial_backward,
    radial_eigenvalues,
):
    highest_mode = lax.Precision.HIGHEST
    fields, slab_points, radial_block, axial_points = forcing.shape
    mode_processors = lax.axis_size("modes")
    radial_devices = lax.axis_size("rad")
    total_theta = slab_points * mode_processors
    retained = radial_forward.shape[0] * mode_processors * radial_devices
    table_upper, table_lower = azimuthal_tables(retained, total_theta)
    flat_values = forcing.reshape(fields, slab_points, radial_block * axial_points)
    columns = lax.all_to_all(flat_values, "modes", split_axis=2, concat_axis=1, tiled=True)
    first = jnp.einsum("kt,ftc->fkc", table_upper, columns, preferred_element_type=jnp.float32)
    second = jnp.einsum("kt,ftc->fkc", table_lower, columns, preferred_element_type=jnp.float32)
    spectral = lax.all_to_all(first + second, "modes", split_axis=1, concat_axis=2, tiled=True)
    local_modes = spectral.shape[1] // 2
    spectral = spectral.reshape(fields, local_modes, 2, radial_block, axial_points)
    axial_coef = jnp.einsum("fmcrz,qz->fmcrq", spectral, axial_forward, precision=highest_mode)
    exchanged = lax.all_to_all(axial_coef, "rad", split_axis=4, concat_axis=3, tiled=True)
    forward_rows, backward_rows, eigen_rows = (
        lax.all_gather(radial_forward, "rad", axis=0, tiled=True),
        lax.all_gather(radial_backward, "rad", axis=0, tiled=True),
        lax.all_gather(radial_eigenvalues, "rad", axis=0, tiled=True),
    )
    axial_block = axial_points // radial_devices
    axial_part = lax.dynamic_slice_in_dim(
        axial_eigenvalues, lax.axis_index("rad") * axial_block, axial_block
    )
    solved = modal_solve(exchanged, forward_rows, backward_rows, eigen_rows, axial_part, diffusion)
    returned = lax.all_to_all(solved, "rad", split_axis=3, concat_axis=4, tiled=True)
    return jnp.einsum("fmcrq,zq->fmcrz", returned, axial_inverse_map, precision=highest_mode)


def per_device(forcing, diffusion, axial_forward, *maps):
    processors, radial_devices = lax.axis_size("modes"), lax.axis_size("rad")
    _, slab, radial_block, width = forcing.shape
    own_modes = maps[2].shape[0]
    paired = (
        radial_devices == 2
        and processors >= 8
        and processors & (processors - 1) == 0
        and radial_block == 8 * processors
        and width % 128 == 0
        and own_modes == 4
        and slab % 32 == 0
        and slab * processors == 8 * own_modes * processors * radial_devices
    )
    plan = paired_plan if paired else general_plan
    return plan(forcing, diffusion, axial_forward, *maps)


def solution(mesh):
    in_specs = (
        P(None, "modes", "rad", None),
        P(),
        P(),
        P(),
        P(),
        P(("modes", "rad"), None, None),
        P(("modes", "rad"), None, None),
        P(("modes", "rad"), None),
    )
    out_specs = P(None, "modes", None, "rad", None)
    return jax.shard_map(
        per_device, mesh=mesh, in_specs=in_specs, out_specs=out_specs, check_vma=False
    )
```

```python
import functools
import math

import jax
import jax.numpy as jnp
import numpy as np
from jax import lax
from jax.experimental import pallas as pl
from jax.experimental.pallas import tpu as pltpu
from jax.sharding import PartitionSpec as P

BF16 = jnp.bfloat16
F32 = jnp.float32
VMEM_BYTES = 40 * 1024 * 1024

CODE_SPAN = 126.0
CODE_MID = 0.5
LN2 = math.log(2.0)
DECODE_SLOPE = 1.0 / (LN2 * CODE_SPAN)
DECODE_SHIFT = CODE_MID / CODE_SPAN
TINY = 1e-35


def code_scale(largest):
    return (largest * 1.008).astype(BF16).astype(F32)


def linear_encode(values, scale):
    inverse = jnp.where(scale > TINY, CODE_SPAN / jnp.maximum(scale, TINY), 0.0)
    return jnp.exp2(values * inverse + CODE_MID)


def linear_decode(coded, scale):
    return scale * (jnp.log(coded) * DECODE_SLOPE - DECODE_SHIFT)


def window_basis(window, total, band, rank):
    points = np.arange(window)
    inner = np.arange(1, window)
    diagonal = np.cos(np.pi * (2 * points - window + 1) / total) * np.cos(np.pi * band / total)
    beside = -np.sin(np.pi * inner / total) * np.sin(np.pi * (window - inner) / total)
    _, vectors = np.linalg.eigh(np.diag(diagonal) + np.diag(beside, 1) + np.diag(beside, -1))
    basis = vectors[:, :rank]
    signs = np.where(np.sum(basis * (points + 0.37)[:, None] ** 2, axis=0) < 0, -1.0, 1.0)
    return basis * signs


def waves(modes, points, total):
    return np.exp(-2j * np.pi * (modes[:, None] * points[None, :] % total) / total)


def interleave(values):
    return np.stack([values.real, values.imag], axis=1).reshape(-1, values.shape[-1])


def half_tables(total, retained, basis, sent):
    window = basis.shape[0]
    half, own = total // 2, retained // 2
    rank = basis.shape[1]
    envelope = window_basis(half, total, own, sent // 2)
    local, join = [], []
    for side in range(2):
        points = side * half + np.arange(half)
        away = (1 - side) * own + np.arange(own)
        centre = (1 - side) * own + 0.5 * (own - 1)
        direct = waves(side * own + np.arange(own), points, total) / np.sqrt(total)
        carried = np.exp(-2j * np.pi * centre * points / total)[None, :] * envelope.T
        rows = np.concatenate([interleave(direct), interleave(carried)])
        rows = rows.reshape(rows.shape[0], -1, window) @ basis
        table = np.zeros((2 * own + sent, half // window, rank + 1))
        table[: rows.shape[0], :, :rank] = rows
        local.append(table)
        offsets = np.exp(-2j * np.pi * (away - centre)[:, None] * points[None, :] / total)
        weights = (offsets @ envelope) / np.sqrt(total)
        parts = np.zeros((own, 2, sent))
        count = 2 * weights.shape[1]
        parts[:, 0, 0:count:2], parts[:, 0, 1:count:2] = weights.real, -weights.imag
        parts[:, 1, 0:count:2], parts[:, 1, 1:count:2] = weights.imag, weights.real
        join.append(parts.reshape(2 * own, sent))
    return np.stack(local), np.stack(join[::-1])


def halves(table):
    upper = table.astype(np.float32).astype(jnp.bfloat16)
    lower = (table - upper.astype(np.float64)).astype(np.float32).astype(jnp.bfloat16)
    return upper, lower


def split(values):
    upper = values.astype(BF16)
    return upper, (values - upper.astype(F32)).astype(BF16)


def dot3(left, right, contract=((1,), (0,))):
    dims = (contract, ((), ()))
    dot = functools.partial(lax.dot_general, dimension_numbers=dims, preferred_element_type=F32)
    return dot(left[0], right[0]) + (dot(left[0], right[1]) + dot(left[1], right[0]))


ROWS_BY_ROWS = ((1,), (1,))


def encode_columns(values, kept):
    scale = code_scale(jnp.max(jnp.abs(values), axis=1, keepdims=True))
    place = lax.broadcasted_iota(jnp.int32, values.shape, 1)
    return jnp.where(place == kept - 1, scale, linear_encode(values, scale))


def decode_columns(coded, kept):
    values = linear_decode(coded, coded[:, kept - 1 : kept, :])
    place = lax.broadcasted_iota(jnp.int32, values.shape, 1)
    return jnp.where(place == kept - 1, 0.0, values)


def rows_body(_, forcing_ref, __, out_ref):
    out_ref[...] = forcing_ref[0]


def encode_body(
    _, own_upper, own_lower, other_upper, other_lower, own_ref, other_ref, __, *out_refs, group, kept
):
    step = pl.program_id(0)
    points, rows, width = other_ref.shape
    blocks = (own_ref[0].astype(F32), other_ref[...].astype(F32))
    tables = ((own_upper[0], own_lower[0]), (other_upper[0], other_lower[0]))
    made = []
    for part in range(rows // group):
        sums = None
        for block, table in zip(blocks, tables):
            piece = block[:, part * group : (part + 1) * group, :].reshape(points * group, width)
            piece = piece.astype(BF16)
            for half in table:
                term = jnp.dot(half, piece, preferred_element_type=F32)
                sums = term if sums is None else sums + term
        coded = encode_columns(sums.reshape(group, kept, width), kept)
        made.append(coded.reshape(group * kept, width).astype(BF16))
    coded = jnp.concatenate(made, axis=0)
    for place, out_ref in enumerate(out_refs):

        @pl.when(step == place)
        def _(out_ref=out_ref):
            out_ref[...] = coded


def gather_body(_, upper_ref, lower_ref, *refs, kept, rows):
    *in_refs, __, own_ref, send_ref, scale_ref = refs
    step = pl.program_id(0)
    width = send_ref.shape[1]
    table = (upper_ref[0], lower_ref[0])
    own = own_ref.shape[1]
    made = []
    for row in range(rows):
        here = slice(row * kept, (row + 1) * kept)
        coded = jnp.stack([ref[here, :].astype(F32) for ref in in_refs])
        sums = dot3(table, split(decode_columns(coded, kept).reshape(-1, width)))
        own_ref[row] = sums[:own]
        scale = code_scale(jnp.max(jnp.abs(sums[own:]), axis=0, keepdims=True))
        scale_ref[pl.ds(step * rows + row, 1), :] = scale
        made.append(linear_encode(sums[own:], scale))
    made = jnp.concatenate(made, axis=0).astype(BF16)
    count = made.shape[0]
    send_ref[pl.ds(pl.multiple_of(step * count, count), count), :] = made

    @pl.when(step == pl.num_programs(0) - 1)
    def _():
        send_ref[send_ref.shape[0] - scale_ref.shape[0] :, :] = scale_ref[...].astype(BF16)


def join_body(
    _, upper_ref, lower_ref, axial_ref, own_ref, in_ref, __, out_ref, held_ref, *, sent, rows
):
    step = pl.program_id(0)
    owners, coded_rows, width = out_ref.shape
    block = coded_rows - 16
    table = (upper_ref[0], lower_ref[0])
    axial = split(axial_ref[...])
    total = in_ref.shape[0] // (sent + 1)
    count = rows * sent
    coded = in_ref[pl.ds(pl.multiple_of(step * count, count), count), :].astype(F32)
    scales = in_ref[total * sent :, :].astype(F32)
    place = lax.broadcasted_iota(jnp.int32, scales.shape, 0)
    for row in range(rows):
        here = place == step * rows + row
        scale = jnp.sum(jnp.where(here, scales, 0.0), axis=0, keepdims=True)
        values = linear_decode(coded[row * sent : (row + 1) * sent], scale)
        spectrum = own_ref[row] + dot3(table, split(values))
        axial_coef = dot3(split(spectrum), axial, ROWS_BY_ROWS).reshape(owners, -1, width)
        each = axial_coef.shape[1]
        target = pl.multiple_of((step * rows + row) * each, each)
        held_ref[:, pl.ds(target, each), :] = axial_coef

    @pl.when(step == pl.num_programs(0) - 1)
    def _():
        for owner in range(owners):
            values = held_ref[owner]
            scale = code_scale(jnp.max(jnp.abs(values), axis=0, keepdims=True))
            out_ref[owner, :block, :] = linear_encode(values, scale).astype(BF16)
            out_ref[owner, block:, :] = jnp.broadcast_to(scale, (16, width)).astype(BF16)


def solve_body(
    place_ref,
    diffusion_ref,
    axial_eigen_ref,
    radial_eigen_ref,
    axial_ref,
    forward_ref,
    backward_ref,
    in_ref,
    *rest,
    field,
    radial_devices,
    modes,
    first_mode,
):
    out_ref, send_ref, held_ref = rest[-3:]
    step = pl.program_id(0)
    each = forward_ref.shape[0]
    devices, coded_rows, width = in_ref.shape
    rows = coded_rows - 16
    chips = devices // radial_devices // 2
    stride = 2 * modes

    @pl.when(step == 0)
    def _():
        for source in range(devices):
            chip, core, block = source // radial_devices // 2, source // radial_devices % 2, source % radial_devices
            target = (block * 2 + core) * chips + chip
            coded = in_ref[source].astype(F32)
            values = linear_decode(coded[:rows], coded[rows : rows + 1])
            for lane in range(width // 128):
                held_ref[lane, target * rows : (target + 1) * rows, :] = values[
                    :, lane * 128 : (lane + 1) * 128
                ]

    radial = devices * rows // stride
    axial = split(axial_ref[...])
    first = place_ref[0] == 0
    for mode in range(each):
        columns = []
        for part in range(2):
            for lane in range(width // 128):
                start = (first_mode + step * each + mode) * 2 + part
                columns.append(held_ref[lane, pl.ds(start, radial, stride=stride), :])
        values = jnp.concatenate(columns, axis=1)
        values = dot3(split(forward_ref[mode]), split(values))
        eigen = jnp.broadcast_to(radial_eigen_ref[mode], (128, radial)).T[:, :1]
        denominator = 1.0 + diffusion_ref[field] * (eigen + axial_eigen_ref[...])
        inverse = 1.0 / denominator
        values = jnp.concatenate([values[:, :width] * inverse, values[:, width:] * inverse], axis=1)
        values = dot3(split(backward_ref[mode]), split(values))
        values = jnp.concatenate([values[:, :width], values[:, width:]], axis=0)
        values = dot3(split(values), axial, ROWS_BY_ROWS)
        values = values.reshape(2, radial_devices, radial // radial_devices, width)
        out_ref[0, mode] = jnp.where(first, values[:, 0], values[:, 1])
        other = jnp.where(first, values[:, 1], values[:, 0]).reshape(radial, width)
        scale = code_scale(jnp.max(jnp.abs(other), axis=0, keepdims=True))
        send_ref[mode, :radial, :] = linear_encode(other, scale).astype(BF16)
        send_ref[mode, radial:, :] = jnp.broadcast_to(scale, (16, width)).astype(BF16)


def finish_body(place_ref, in_ref, _, __, out_ref):
    radial = out_ref.shape[2] * out_ref.shape[3]
    for mode in range(in_ref.shape[0]):
        coded = in_ref[mode].astype(F32)
        values = linear_decode(coded[:radial], coded[radial : radial + 1])
        out_ref[0, mode] = values.reshape(out_ref.shape[2:])


def params():
    return pltpu.CompilerParams(
        vmem_limit_bytes=VMEM_BYTES, dimension_semantics=("arbitrary",)
    )


def cost(microseconds):
    return pl.CostEstimate(
        flops=int(microseconds * 3e10), bytes_accessed=int(microseconds * 3e8), transcendentals=0
    )


def whole(shape):
    return pl.BlockSpec(shape, lambda *_: (0,) * len(shape))


SMEM = pl.BlockSpec(memory_space=pltpu.SMEM)
ANY = pl.BlockSpec(memory_space=pl.ANY)


def paired_plan(
    forcing,
    diffusion,
    axial_forward,
    axial_inverse_map,
    axial_eigenvalues,
    radial_forward,
    radial_backward,
    radial_eigenvalues,
):
    fields, slab, radial_block, width = forcing.shape
    processors, radial_devices = lax.axis_size("modes"), lax.axis_size("rad")
    devices = processors * radial_devices
    total, radial = slab * processors, radial_block * radial_devices
    own_modes = radial_forward.shape[0]
    retained = own_modes * devices
    near = processors // 2
    owners = near * radial_devices
    rows = radial_block // near
    group, kept, sent = 8, slab * 3 // 4, 88
    per_owner = 2 * own_modes
    chips = near // 2
    position = lax.axis_index("modes")
    core, chip, side = position % 2, position // 2 % chips, position // near
    place = jnp.stack([lax.axis_index("rad"), side, core, chip, side * chips + chip]).astype(jnp.int32)

    window = 2 * slab
    basis = window_basis(window, total, 2 * retained - 1, kept - 1)
    spread = np.zeros((2, group, kept, slab, group))
    for row in range(group):
        spread[:, row, : kept - 1, :, row] = basis.reshape(2, slab, kept - 1).transpose(0, 2, 1)
    spread_upper, spread_lower = halves(spread.reshape(2, group * kept, slab * group))
    local, join_table = half_tables(total, retained, basis, sent)
    seen = [[here ^ step for step in range(chips)] for here in range(chips)]
    local = np.stack([table[:, order] for table in local for order in seen])
    local_upper, local_lower = halves(local.reshape(2 * chips, retained + sent, chips * kept))
    join_upper, join_lower = halves(join_table)
    axial_eigen = axial_eigenvalues.reshape(1, width)
    radial_eigen = radial_eigenvalues.reshape(own_modes, 1, radial)

    def chosen(table, index):
        return pl.BlockSpec((1,) + table.shape[1:], lambda i, p: (index(p), 0, 0))

    def encode(field, targets, other, after):
        message = (rows * kept, width)
        first = targets[0]
        return pl.pallas_call(
            functools.partial(encode_body, group=group, kept=kept),
            grid_spec=pltpu.PrefetchScalarGridSpec(
                num_scalar_prefetch=1,
                grid=(len(targets),),
                in_specs=[
                    chosen(spread_upper, lambda p: p[2]),
                    chosen(spread_lower, lambda p: p[2]),
                    chosen(spread_upper, lambda p: 1 - p[2]),
                    chosen(spread_lower, lambda p: 1 - p[2]),
                    pl.BlockSpec(
                        (1, slab, rows, width), lambda i, p: (field, 0, p[2] * chips + (p[3] ^ (first + i)), 0)
                    ),
                    pl.BlockSpec((slab, rows, width), lambda i, p: (0, (p[3] ^ (first + i)), 0)),
                    ANY,
                ],
                out_specs=[whole(message)] * len(targets),
            ),
            out_shape=[jax.ShapeDtypeStruct(message, BF16)] * len(targets),
            compiler_params=params(),
            cost_estimate=cost(7),
            name="window_coefficients",
        )(
            place,
            jnp.asarray(spread_upper),
            jnp.asarray(spread_lower),
            jnp.asarray(spread_upper),
            jnp.asarray(spread_lower),
            forcing,
            other,
            after,
        )

    def gather(received, after):
        step = 8
        message = (rows * (sent + 1), width)
        return pl.pallas_call(
            functools.partial(gather_body, kept=kept, rows=step),
            grid_spec=pltpu.PrefetchScalarGridSpec(
                num_scalar_prefetch=1,
                grid=(rows // step,),
                in_specs=[chosen(local_upper, lambda p: p[4]), chosen(local_lower, lambda p: p[4])]
                + [pl.BlockSpec((step * kept, width), lambda i, _: (i, 0))] * chips
                + [ANY],
                out_specs=[
                    pl.BlockSpec((step, retained, width), lambda i, _: (i, 0, 0)),
                    whole(message),
                ],
                scratch_shapes=[pltpu.VMEM((rows, width), F32)],
            ),
            out_shape=[
                jax.ShapeDtypeStruct((rows, retained, width), F32),
                jax.ShapeDtypeStruct(message, BF16),
            ],
            compiler_params=params(),
            cost_estimate=cost(5),
            name="half_sums",
        )(place, jnp.asarray(local_upper), jnp.asarray(local_lower), *received, after)

    def join(own, received, after):
        step = 8
        block = rows * per_owner
        return pl.pallas_call(
            functools.partial(join_body, sent=sent, rows=step),
            grid_spec=pltpu.PrefetchScalarGridSpec(
                num_scalar_prefetch=1,
                grid=(rows // step,),
                in_specs=[
                    chosen(join_upper, lambda p: p[1]),
                    chosen(join_lower, lambda p: p[1]),
                    whole(axial_forward.shape),
                    pl.BlockSpec((step, retained, width), lambda i, _: (i, 0, 0)),
                    whole(received.shape),
                    ANY,
                ],
                out_specs=whole((owners, block + 16, width)),
                scratch_shapes=[pltpu.VMEM((owners, block, width), F32)],
            ),
            out_shape=jax.ShapeDtypeStruct((owners, block + 16, width), BF16),
            compiler_params=params(),
            cost_estimate=cost(6),
            name="modal_axial_coefficients",
        )(
            place,
            jnp.asarray(join_upper),
            jnp.asarray(join_lower),
            axial_forward,
            own,
            received,
            after,
        )

    out_shape = jax.ShapeDtypeStruct((fields, own_modes * radial_devices, 2, radial_block, width), F32)
    each = 2
    turns = own_modes // each
    out_block = (1, each, 2, radial_block, width)
    send_rows = radial + 16

    def solve(field, modes, received, out, after):
        carried = [] if out is None else [out]
        begin = modes[0] // each
        count = len(modes) // each
        return pl.pallas_call(
            functools.partial(
                solve_body,
                field=field,
                radial_devices=radial_devices,
                modes=own_modes,
                first_mode=modes[0],
            ),
            grid_spec=pltpu.PrefetchScalarGridSpec(
                num_scalar_prefetch=1,
                grid=(count,),
                in_specs=[
                    SMEM,
                    whole(axial_eigen.shape),
                    pl.BlockSpec((each, 1, radial), lambda i, _: (begin + i, 0, 0)),
                    whole(axial_inverse_map.shape),
                    pl.BlockSpec((each, radial, radial), lambda i, _: (begin + i, 0, 0)),
                    pl.BlockSpec((each, radial, radial), lambda i, _: (begin + i, 0, 0)),
                    whole(received.shape),
                ]
                + [ANY] * (1 + len(carried)),
                out_specs=[
                    pl.BlockSpec(out_block, lambda i, y: (field, y[0] * turns + begin + i, 0, 0, 0)),
                    pl.BlockSpec((each, send_rows, width), lambda i, _: (i, 0, 0)),
                ],
                scratch_shapes=[pltpu.VMEM((width // 128, radial * per_owner, 128), F32)],
            ),
            out_shape=[out_shape, jax.ShapeDtypeStruct((len(modes), send_rows, width), BF16)],
            input_output_aliases={9: 0} if carried else {},
            compiler_params=params(),
            cost_estimate=cost(7),
            name="radial_solve",
        )(
            place,
            diffusion,
            axial_eigen,
            radial_eigen,
            axial_inverse_map,
            radial_forward,
            radial_backward,
            received,
            after,
            *carried,
        )

    def finish(field, modes, received, out, after):
        begin = modes[0] // each
        return pl.pallas_call(
            finish_body,
            grid_spec=pltpu.PrefetchScalarGridSpec(
                num_scalar_prefetch=1,
                grid=(len(modes) // each,),
                in_specs=[
                    pl.BlockSpec((each, send_rows, width), lambda i, _: (i, 0, 0)),
                    ANY,
                    ANY,
                ],
                out_specs=pl.BlockSpec(
                    out_block, lambda i, y: (field, (1 - y[0]) * turns + begin + i, 0, 0, 0)
                ),
            ),
            out_shape=out_shape,
            input_output_aliases={2: 0},
            compiler_params=params(),
            cost_estimate=cost(2),
            name="partner_rows",
        )(place, received, out, after)

    side_owners = [list(range(owners)), list(range(owners, 2 * owners))]

    def exchange(values, names, groups):
        return lax.all_to_all(
            values, names, split_axis=0, concat_axis=0, tiled=True, axis_index_groups=groups
        )

    def flip(values, bits):
        return lax.ppermute(values, "modes", [(i, i ^ bits) for i in range(processors)])

    def other_rows(field, after):
        shape = (slab, radial_block // 2, width)
        return pl.pallas_call(
            rows_body,
            grid_spec=pltpu.PrefetchScalarGridSpec(
                num_scalar_prefetch=1,
                grid=(2,),
                in_specs=[
                    pl.BlockSpec(
                        (1, slab // 2) + shape[1:], lambda i, p: (field, i, 1 - p[2], 0)
                    ),
                    ANY,
                ],
                out_specs=pl.BlockSpec((slab // 2,) + shape[1:], lambda i, _: (i, 0, 0)),
            ),
            out_shape=jax.ShapeDtypeStruct(shape, BF16),
            compiler_params=params(),
            cost_estimate=cost(2),
            name="other_core_rows",
        )(place, forcing, after)

    def partner(values):
        return lax.ppermute(values, "rad", [(0, 1), (1, 0)])

    places = tuple(range(chips))
    every = tuple(range(own_modes))
    head, tail = every[: own_modes // 2], every[own_modes // 2 :]
    steps = [
        ("rows", 0, None),
        ("rows", 1, None),
        ("encode", 0, places),
        ("rows", 2, None),
        ("encode", 1, places),
        ("gather", 0, None),
        ("encode", 2, places),
        ("gather", 1, None),
        ("join", 0, None),
        ("gather", 2, None),
        ("join", 1, None),
        ("solve", 0, every),
        ("join", 2, None),
        ("solve", 1, every),
        ("finish", 0, every),
        ("solve", 2, head),
        ("solve", 2, tail),
        ("finish", 1, every),
        ("finish", 2, head),
        ("finish", 2, tail),
    ]
    swapped, own, away, spectra, partners = {}, {}, {}, {}, {}
    windows = {field: {} for field in range(fields)}
    last, out = diffusion, None
    for name, field, which in steps:
        key = (field, which)
        if name == "rows":
            last = other_rows(field, last)
            swapped[field] = flip(last, 1)
        elif name == "encode":
            made = encode(field, which, swapped[field], last)
            last = made[0]
            for target, message in zip(which, made):
                windows[field][target] = flip(message, 2 * target) if target else message
        elif name == "gather":
            own[field], last = gather([windows[field][j] for j in range(chips)], last)
            away[field] = flip(last, near)
        elif name == "join":
            last = join(own[field], away[field], last)
            spectra[field] = exchange(last, ("modes", "rad"), side_owners)
        elif name == "solve":
            out, last = solve(field, which, spectra[field], out, last)
            partners[key] = partner(last)
        else:
            out = finish(field, which, partners[key], out, last)
    return out


def azimuthal_tables(retained, points):
    row_index = jnp.arange(2 * retained, dtype=jnp.int32)
    wavenumber = row_index // 2
    quarter = (row_index % 2).astype(jnp.float32) * (0.5 * math.pi)
    theta_index = jnp.arange(points, dtype=jnp.int32)
    phase_index = wavenumber[:, None] * theta_index[None, :] % points
    radians = phase_index.astype(jnp.float32) * (2.0 * math.pi / points) + quarter[:, None]
    table = jnp.cos(radians) * (1.0 / math.sqrt(points))
    upper = table.astype(jnp.bfloat16)
    widened = lax.optimization_barrier(upper).astype(jnp.float32)
    lower = (table - widened).astype(jnp.bfloat16)
    return (upper, lower)


def modal_solve(spectral_coefficients, forward_map, backward, eigenvalues, axial_part, diffusion):
    highest_mode = lax.Precision.HIGHEST
    radial_coefficients = jnp.einsum(
        "hzv,bhtvp->bhtzp", forward_map, spectral_coefficients, precision=highest_mode
    )
    denominator = 1.0 + diffusion[:, None, None, None, None] * (
        eigenvalues[None, :, None, :, None] + axial_part[None, None, None, None, :]
    )
    return jnp.einsum(
        "mri,fmciq->fmcrq", backward, radial_coefficients / denominator, precision=highest_mode
    )


def general_plan(
    forcing,
    diffusion,
    axial_forward,
    axial_inverse_map,
    axial_eigenvalues,
    radial_forward,
    radial_backward,
    radial_eigenvalues,
):
    highest_mode = lax.Precision.HIGHEST
    fields, slab_points, radial_block, axial_points = forcing.shape
    mode_processors = lax.axis_size("modes")
    radial_devices = lax.axis_size("rad")
    total_theta = slab_points * mode_processors
    retained = radial_forward.shape[0] * mode_processors * radial_devices
    table_upper, table_lower = azimuthal_tables(retained, total_theta)
    flat_values = forcing.reshape(fields, slab_points, radial_block * axial_points)
    columns = lax.all_to_all(flat_values, "modes", split_axis=2, concat_axis=1, tiled=True)
    first = jnp.einsum("kt,ftc->fkc", table_upper, columns, preferred_element_type=jnp.float32)
    second = jnp.einsum("kt,ftc->fkc", table_lower, columns, preferred_element_type=jnp.float32)
    spectral = lax.all_to_all(first + second, "modes", split_axis=1, concat_axis=2, tiled=True)
    local_modes = spectral.shape[1] // 2
    spectral = spectral.reshape(fields, local_modes, 2, radial_block, axial_points)
    axial_coef = jnp.einsum("fmcrz,qz->fmcrq", spectral, axial_forward, precision=highest_mode)
    exchanged = lax.all_to_all(axial_coef, "rad", split_axis=4, concat_axis=3, tiled=True)
    forward_rows, backward_rows, eigen_rows = (
        lax.all_gather(radial_forward, "rad", axis=0, tiled=True),
        lax.all_gather(radial_backward, "rad", axis=0, tiled=True),
        lax.all_gather(radial_eigenvalues, "rad", axis=0, tiled=True),
    )
    axial_block = axial_points // radial_devices
    axial_part = lax.dynamic_slice_in_dim(
        axial_eigenvalues, lax.axis_index("rad") * axial_block, axial_block
    )
    solved = modal_solve(exchanged, forward_rows, backward_rows, eigen_rows, axial_part, diffusion)
    returned = lax.all_to_all(solved, "rad", split_axis=3, concat_axis=4, tiled=True)
    return jnp.einsum("fmcrq,zq->fmcrz", returned, axial_inverse_map, precision=highest_mode)


def per_device(forcing, diffusion, axial_forward, *maps):
    processors, radial_devices = lax.axis_size("modes"), lax.axis_size("rad")
    _, slab, radial_block, width = forcing.shape
    own_modes = maps[2].shape[0]
    paired = (
        radial_devices == 2
        and processors >= 8
        and processors & (processors - 1) == 0
        and radial_block == 8 * processors
        and width % 128 == 0
        and own_modes == 4
        and slab % 32 == 0
        and slab * processors == 8 * own_modes * processors * radial_devices
    )
    plan = paired_plan if paired else general_plan
    return plan(forcing, diffusion, axial_forward, *maps)


def solution(mesh):
    in_specs = (
        P(None, "modes", "rad", None),
        P(),
        P(),
        P(),
        P(),
        P(("modes", "rad"), None, None),
        P(("modes", "rad"), None, None),
        P(("modes", "rad"), None),
    )
    out_specs = P(None, "modes", None, "rad", None)
    return jax.shard_map(
        per_device, mesh=mesh, in_specs=in_specs, out_specs=out_specs, check_vma=False
    )
```

```python
import functools
import math

import jax
import jax.numpy as jnp
import numpy as np
from jax import lax
from jax.experimental import pallas as pl
from jax.experimental.pallas import tpu as pltpu
from jax.sharding import PartitionSpec as P

BF16 = jnp.bfloat16
F32 = jnp.float32
VMEM_BYTES = 40 * 1024 * 1024

CODE_SPAN = 126.0
CODE_MID = 0.5
LN2 = math.log(2.0)
DECODE_SLOPE = 1.0 / (LN2 * CODE_SPAN)
DECODE_SHIFT = CODE_MID / CODE_SPAN
TINY = 1e-35


def code_scale(largest):
    return (largest * 1.008).astype(BF16).astype(F32)


def linear_encode(values, scale):
    inverse = jnp.where(scale > TINY, CODE_SPAN / jnp.maximum(scale, TINY), 0.0)
    return jnp.exp2(values * inverse + CODE_MID)


def linear_decode(coded, scale):
    return scale * (jnp.log(coded) * DECODE_SLOPE - DECODE_SHIFT)


def window_basis(window, total, band, rank):
    points = np.arange(window)
    inner = np.arange(1, window)
    diagonal = np.cos(np.pi * (2 * points - window + 1) / total) * np.cos(np.pi * band / total)
    beside = -np.sin(np.pi * inner / total) * np.sin(np.pi * (window - inner) / total)
    _, vectors = np.linalg.eigh(np.diag(diagonal) + np.diag(beside, 1) + np.diag(beside, -1))
    basis = vectors[:, :rank]
    signs = np.where(np.sum(basis * (points + 0.37)[:, None] ** 2, axis=0) < 0, -1.0, 1.0)
    return basis * signs


def waves(modes, points, total):
    return np.exp(-2j * np.pi * (modes[:, None] * points[None, :] % total) / total)


def interleave(values):
    return np.stack([values.real, values.imag], axis=1).reshape(-1, values.shape[-1])


def half_tables(total, retained, basis, sent):
    window = basis.shape[0]
    half, own = total // 2, retained // 2
    rank = basis.shape[1]
    envelope = window_basis(half, total, own, sent // 2)
    local, join = [], []
    for side in range(2):
        points = side * half + np.arange(half)
        away = (1 - side) * own + np.arange(own)
        centre = (1 - side) * own + 0.5 * (own - 1)
        direct = waves(side * own + np.arange(own), points, total) / np.sqrt(total)
        carried = np.exp(-2j * np.pi * centre * points / total)[None, :] * envelope.T
        rows = np.concatenate([interleave(direct), interleave(carried)])
        rows = rows.reshape(rows.shape[0], -1, window) @ basis
        table = np.zeros((2 * own + sent, half // window, rank + 1))
        table[: rows.shape[0], :, :rank] = rows
        local.append(table)
        offsets = np.exp(-2j * np.pi * (away - centre)[:, None] * points[None, :] / total)
        weights = (offsets @ envelope) / np.sqrt(total)
        parts = np.zeros((own, 2, sent))
        count = 2 * weights.shape[1]
        parts[:, 0, 0:count:2], parts[:, 0, 1:count:2] = weights.real, -weights.imag
        parts[:, 1, 0:count:2], parts[:, 1, 1:count:2] = weights.imag, weights.real
        join.append(parts.reshape(2 * own, sent))
    return np.stack(local), np.stack(join[::-1])


def halves(table):
    upper = table.astype(np.float32).astype(jnp.bfloat16)
    lower = (table - upper.astype(np.float64)).astype(np.float32).astype(jnp.bfloat16)
    return upper, lower


def split(values):
    upper = values.astype(BF16)
    return upper, (values - upper.astype(F32)).astype(BF16)


def dot3(left, right, contract=((1,), (0,))):
    dims = (contract, ((), ()))
    dot = functools.partial(lax.dot_general, dimension_numbers=dims, preferred_element_type=F32)
    return dot(left[0], right[0]) + (dot(left[0], right[1]) + dot(left[1], right[0]))


ROWS_BY_ROWS = ((1,), (1,))


def encode_columns(values, kept):
    scale = code_scale(jnp.max(jnp.abs(values), axis=1, keepdims=True))
    place = lax.broadcasted_iota(jnp.int32, values.shape, 1)
    return jnp.where(place == kept - 1, scale, linear_encode(values, scale))


def decode_columns(coded, kept):
    values = linear_decode(coded, coded[:, kept - 1 : kept, :])
    place = lax.broadcasted_iota(jnp.int32, values.shape, 1)
    return jnp.where(place == kept - 1, 0.0, values)


def rows_body(_, forcing_ref, __, out_ref):
    out_ref[...] = forcing_ref[0]


def encode_body(
    _, own_upper, own_lower, other_upper, other_lower, own_ref, other_ref, __, *out_refs, group, kept
):
    step = pl.program_id(0)
    points, rows, width = other_ref.shape
    blocks = (own_ref[0].astype(F32), other_ref[...].astype(F32))
    tables = ((own_upper[0], own_lower[0]), (other_upper[0], other_lower[0]))
    made = []
    for part in range(rows // group):
        sums = None
        for block, table in zip(blocks, tables):
            piece = block[:, part * group : (part + 1) * group, :].reshape(points * group, width)
            piece = piece.astype(BF16)
            for half in table:
                term = jnp.dot(half, piece, preferred_element_type=F32)
                sums = term if sums is None else sums + term
        coded = encode_columns(sums.reshape(group, kept, width), kept)
        made.append(coded.reshape(group * kept, width).astype(BF16))
    coded = jnp.concatenate(made, axis=0)
    for place, out_ref in enumerate(out_refs):

        @pl.when(step == place)
        def _(out_ref=out_ref):
            out_ref[...] = coded


def gather_body(_, upper_ref, lower_ref, *refs, kept, rows):
    *in_refs, __, own_ref, send_ref, scale_ref = refs
    step = pl.program_id(0)
    width = send_ref.shape[1]
    table = (upper_ref[0], lower_ref[0])
    own = own_ref.shape[1]
    made = []
    for row in range(rows):
        here = slice(row * kept, (row + 1) * kept)
        coded = jnp.stack([ref[here, :].astype(F32) for ref in in_refs])
        sums = dot3(table, split(decode_columns(coded, kept).reshape(-1, width)))
        own_ref[row] = sums[:own]
        scale = code_scale(jnp.max(jnp.abs(sums[own:]), axis=0, keepdims=True))
        scale_ref[pl.ds(step * rows + row, 1), :] = scale
        made.append(linear_encode(sums[own:], scale))
    made = jnp.concatenate(made, axis=0).astype(BF16)
    count = made.shape[0]
    send_ref[pl.ds(pl.multiple_of(step * count, count), count), :] = made

    @pl.when(step == pl.num_programs(0) - 1)
    def _():
        send_ref[send_ref.shape[0] - scale_ref.shape[0] :, :] = scale_ref[...].astype(BF16)


def join_body(
    _, upper_ref, lower_ref, axial_ref, own_ref, in_ref, __, out_ref, held_ref, *, sent, rows
):
    step = pl.program_id(0)
    owners, coded_rows, width = out_ref.shape
    block = coded_rows - 16
    table = (upper_ref[0], lower_ref[0])
    axial = split(axial_ref[...])
    total = in_ref.shape[0] // (sent + 1)
    count = rows * sent
    coded = in_ref[pl.ds(pl.multiple_of(step * count, count), count), :].astype(F32)
    scales = in_ref[total * sent :, :].astype(F32)
    place = lax.broadcasted_iota(jnp.int32, scales.shape, 0)
    for row in range(rows):
        here = place == step * rows + row
        scale = jnp.sum(jnp.where(here, scales, 0.0), axis=0, keepdims=True)
        values = linear_decode(coded[row * sent : (row + 1) * sent], scale)
        spectrum = own_ref[row] + dot3(table, split(values))
        axial_coef = dot3(split(spectrum), axial, ROWS_BY_ROWS).reshape(owners, -1, width)
        each = axial_coef.shape[1]
        target = pl.multiple_of((step * rows + row) * each, each)
        held_ref[:, pl.ds(target, each), :] = axial_coef

    @pl.when(step == pl.num_programs(0) - 1)
    def _():
        for owner in range(owners):
            values = held_ref[owner]
            scale = code_scale(jnp.max(jnp.abs(values), axis=0, keepdims=True))
            out_ref[owner, :block, :] = linear_encode(values, scale).astype(BF16)
            out_ref[owner, block:, :] = jnp.broadcast_to(scale, (16, width)).astype(BF16)


def solve_body(
    place_ref,
    diffusion_ref,
    axial_eigen_ref,
    radial_eigen_ref,
    axial_ref,
    forward_ref,
    backward_ref,
    in_ref,
    *rest,
    field,
    radial_devices,
    modes,
    first_mode,
):
    out_ref, send_ref, held_ref = rest[-3:]
    step = pl.program_id(0)
    each = forward_ref.shape[0]
    devices, coded_rows, width = in_ref.shape
    rows = coded_rows - 16
    chips = devices // radial_devices // 2
    stride = 2 * modes

    @pl.when(step == 0)
    def _():
        for source in range(devices):
            chip, core, block = source // radial_devices // 2, source // radial_devices % 2, source % radial_devices
            target = (block * 2 + core) * chips + chip
            coded = in_ref[source].astype(F32)
            values = linear_decode(coded[:rows], coded[rows : rows + 1])
            for lane in range(width // 128):
                held_ref[lane, target * rows : (target + 1) * rows, :] = values[
                    :, lane * 128 : (lane + 1) * 128
                ]

    radial = devices * rows // stride
    axial = split(axial_ref[...])
    first = place_ref[0] == 0
    for mode in range(each):
        columns = []
        for part in range(2):
            for lane in range(width // 128):
                start = (first_mode + step * each + mode) * 2 + part
                columns.append(held_ref[lane, pl.ds(start, radial, stride=stride), :])
        values = jnp.concatenate(columns, axis=1)
        values = dot3(split(forward_ref[mode]), split(values))
        eigen = jnp.broadcast_to(radial_eigen_ref[mode], (128, radial)).T[:, :1]
        denominator = 1.0 + diffusion_ref[field] * (eigen + axial_eigen_ref[...])
        inverse = 1.0 / denominator
        values = jnp.concatenate([values[:, :width] * inverse, values[:, width:] * inverse], axis=1)
        values = dot3(split(backward_ref[mode]), split(values))
        values = jnp.concatenate([values[:, :width], values[:, width:]], axis=0)
        values = dot3(split(values), axial, ROWS_BY_ROWS)
        values = values.reshape(2, radial_devices, radial // radial_devices, width)
        out_ref[0, mode] = jnp.where(first, values[:, 0], values[:, 1])
        other = jnp.where(first, values[:, 1], values[:, 0]).reshape(radial, width)
        scale = code_scale(jnp.max(jnp.abs(other), axis=0, keepdims=True))
        send_ref[mode, :radial, :] = linear_encode(other, scale).astype(BF16)
        send_ref[mode, radial:, :] = jnp.broadcast_to(scale, (16, width)).astype(BF16)


def finish_body(place_ref, in_ref, _, __, out_ref):
    radial = out_ref.shape[2] * out_ref.shape[3]
    for mode in range(in_ref.shape[0]):
        coded = in_ref[mode].astype(F32)
        values = linear_decode(coded[:radial], coded[radial : radial + 1])
        out_ref[0, mode] = values.reshape(out_ref.shape[2:])


def params():
    return pltpu.CompilerParams(
        vmem_limit_bytes=VMEM_BYTES, dimension_semantics=("arbitrary",)
    )


def cost(microseconds):
    return pl.CostEstimate(
        flops=int(microseconds * 3e10), bytes_accessed=int(microseconds * 3e8), transcendentals=0
    )


def whole(shape):
    return pl.BlockSpec(shape, lambda *_: (0,) * len(shape))


SMEM = pl.BlockSpec(memory_space=pltpu.SMEM)
ANY = pl.BlockSpec(memory_space=pl.ANY)


def paired_plan(
    forcing,
    diffusion,
    axial_forward,
    axial_inverse_map,
    axial_eigenvalues,
    radial_forward,
    radial_backward,
    radial_eigenvalues,
):
    fields, slab, radial_block, width = forcing.shape
    processors, radial_devices = lax.axis_size("modes"), lax.axis_size("rad")
    devices = processors * radial_devices
    total, radial = slab * processors, radial_block * radial_devices
    own_modes = radial_forward.shape[0]
    retained = own_modes * devices
    near = processors // 2
    owners = near * radial_devices
    rows = radial_block // near
    group, kept, sent = 8, slab * 3 // 4, 88
    per_owner = 2 * own_modes
    chips = near // 2
    position = lax.axis_index("modes")
    core, chip, side = position % 2, position // 2 % chips, position // near
    place = jnp.stack([lax.axis_index("rad"), side, core, chip, side * chips + chip]).astype(jnp.int32)

    window = 2 * slab
    basis = window_basis(window, total, 2 * retained - 1, kept - 1)
    spread = np.zeros((2, group, kept, slab, group))
    for row in range(group):
        spread[:, row, : kept - 1, :, row] = basis.reshape(2, slab, kept - 1).transpose(0, 2, 1)
    spread_upper, spread_lower = halves(spread.reshape(2, group * kept, slab * group))
    local, join_table = half_tables(total, retained, basis, sent)
    seen = [[here ^ step for step in range(chips)] for here in range(chips)]
    local = np.stack([table[:, order] for table in local for order in seen])
    local_upper, local_lower = halves(local.reshape(2 * chips, retained + sent, chips * kept))
    join_upper, join_lower = halves(join_table)
    axial_eigen = axial_eigenvalues.reshape(1, width)
    radial_eigen = radial_eigenvalues.reshape(own_modes, 1, radial)

    def chosen(table, index):
        return pl.BlockSpec((1,) + table.shape[1:], lambda i, p: (index(p), 0, 0))

    def encode(field, targets, other, after):
        message = (rows * kept, width)
        first = targets[0]
        return pl.pallas_call(
            functools.partial(encode_body, group=group, kept=kept),
            grid_spec=pltpu.PrefetchScalarGridSpec(
                num_scalar_prefetch=1,
                grid=(len(targets),),
                in_specs=[
                    chosen(spread_upper, lambda p: p[2]),
                    chosen(spread_lower, lambda p: p[2]),
                    chosen(spread_upper, lambda p: 1 - p[2]),
                    chosen(spread_lower, lambda p: 1 - p[2]),
                    pl.BlockSpec(
                        (1, slab, rows, width), lambda i, p: (field, 0, p[2] * chips + (p[3] ^ (first + i)), 0)
                    ),
                    pl.BlockSpec((slab, rows, width), lambda i, p: (0, (p[3] ^ (first + i)), 0)),
                    ANY,
                ],
                out_specs=[whole(message)] * len(targets),
            ),
            out_shape=[jax.ShapeDtypeStruct(message, BF16)] * len(targets),
            compiler_params=params(),
            cost_estimate=cost(7),
            name="window_coefficients",
        )(
            place,
            jnp.asarray(spread_upper),
            jnp.asarray(spread_lower),
            jnp.asarray(spread_upper),
            jnp.asarray(spread_lower),
            forcing,
            other,
            after,
        )

    def gather(received, after):
        step = 8
        message = (rows * (sent + 1), width)
        return pl.pallas_call(
            functools.partial(gather_body, kept=kept, rows=step),
            grid_spec=pltpu.PrefetchScalarGridSpec(
                num_scalar_prefetch=1,
                grid=(rows // step,),
                in_specs=[chosen(local_upper, lambda p: p[4]), chosen(local_lower, lambda p: p[4])]
                + [pl.BlockSpec((step * kept, width), lambda i, _: (i, 0))] * chips
                + [ANY],
                out_specs=[
                    pl.BlockSpec((step, retained, width), lambda i, _: (i, 0, 0)),
                    whole(message),
                ],
                scratch_shapes=[pltpu.VMEM((rows, width), F32)],
            ),
            out_shape=[
                jax.ShapeDtypeStruct((rows, retained, width), F32),
                jax.ShapeDtypeStruct(message, BF16),
            ],
            compiler_params=params(),
            cost_estimate=cost(5),
            name="half_sums",
        )(place, jnp.asarray(local_upper), jnp.asarray(local_lower), *received, after)

    def join(own, received, after):
        step = 8
        block = rows * per_owner
        return pl.pallas_call(
            functools.partial(join_body, sent=sent, rows=step),
            grid_spec=pltpu.PrefetchScalarGridSpec(
                num_scalar_prefetch=1,
                grid=(rows // step,),
                in_specs=[
                    chosen(join_upper, lambda p: p[1]),
                    chosen(join_lower, lambda p: p[1]),
                    whole(axial_forward.shape),
                    pl.BlockSpec((step, retained, width), lambda i, _: (i, 0, 0)),
                    whole(received.shape),
                    ANY,
                ],
                out_specs=whole((owners, block + 16, width)),
                scratch_shapes=[pltpu.VMEM((owners, block, width), F32)],
            ),
            out_shape=jax.ShapeDtypeStruct((owners, block + 16, width), BF16),
            compiler_params=params(),
            cost_estimate=cost(6),
            name="modal_axial_coefficients",
        )(
            place,
            jnp.asarray(join_upper),
            jnp.asarray(join_lower),
            axial_forward,
            own,
            received,
            after,
        )

    out_shape = jax.ShapeDtypeStruct((fields, own_modes * radial_devices, 2, radial_block, width), F32)
    each = 2
    turns = own_modes // each
    out_block = (1, each, 2, radial_block, width)
    send_rows = radial + 16

    def solve(field, modes, received, out, after):
        carried = [] if out is None else [out]
        begin = modes[0] // each
        count = len(modes) // each
        return pl.pallas_call(
            functools.partial(
                solve_body,
                field=field,
                radial_devices=radial_devices,
                modes=own_modes,
                first_mode=modes[0],
            ),
            grid_spec=pltpu.PrefetchScalarGridSpec(
                num_scalar_prefetch=1,
                grid=(count,),
                in_specs=[
                    SMEM,
                    whole(axial_eigen.shape),
                    pl.BlockSpec((each, 1, radial), lambda i, _: (begin + i, 0, 0)),
                    whole(axial_inverse_map.shape),
                    pl.BlockSpec((each, radial, radial), lambda i, _: (begin + i, 0, 0)),
                    pl.BlockSpec((each, radial, radial), lambda i, _: (begin + i, 0, 0)),
                    whole(received.shape),
                ]
                + [ANY] * (1 + len(carried)),
                out_specs=[
                    pl.BlockSpec(out_block, lambda i, y: (field, y[0] * turns + begin + i, 0, 0, 0)),
                    pl.BlockSpec((each, send_rows, width), lambda i, _: (i, 0, 0)),
                ],
                scratch_shapes=[pltpu.VMEM((width // 128, (radial + 1) * per_owner, 128), F32)],
            ),
            out_shape=[out_shape, jax.ShapeDtypeStruct((len(modes), send_rows, width), BF16)],
            input_output_aliases={9: 0} if carried else {},
            compiler_params=params(),
            cost_estimate=cost(7),
            name="radial_solve",
        )(
            place,
            diffusion,
            axial_eigen,
            radial_eigen,
            axial_inverse_map,
            radial_forward,
            radial_backward,
            received,
            after,
            *carried,
        )

    def finish(field, modes, received, out, after):
        begin = modes[0] // each
        return pl.pallas_call(
            finish_body,
            grid_spec=pltpu.PrefetchScalarGridSpec(
                num_scalar_prefetch=1,
                grid=(len(modes) // each,),
                in_specs=[
                    pl.BlockSpec((each, send_rows, width), lambda i, _: (i, 0, 0)),
                    ANY,
                    ANY,
                ],
                out_specs=pl.BlockSpec(
                    out_block, lambda i, y: (field, (1 - y[0]) * turns + begin + i, 0, 0, 0)
                ),
            ),
            out_shape=out_shape,
            input_output_aliases={2: 0},
            compiler_params=params(),
            cost_estimate=cost(2),
            name="partner_rows",
        )(place, received, out, after)

    side_owners = [list(range(owners)), list(range(owners, 2 * owners))]

    def exchange(values, names, groups):
        return lax.all_to_all(
            values, names, split_axis=0, concat_axis=0, tiled=True, axis_index_groups=groups
        )

    def flip(values, bits):
        return lax.ppermute(values, "modes", [(i, i ^ bits) for i in range(processors)])

    def other_rows(field, after):
        shape = (slab, radial_block // 2, width)
        return pl.pallas_call(
            rows_body,
            grid_spec=pltpu.PrefetchScalarGridSpec(
                num_scalar_prefetch=1,
                grid=(2,),
                in_specs=[
                    pl.BlockSpec(
                        (1, slab // 2) + shape[1:], lambda i, p: (field, i, 1 - p[2], 0)
                    ),
                    ANY,
                ],
                out_specs=pl.BlockSpec((slab // 2,) + shape[1:], lambda i, _: (i, 0, 0)),
            ),
            out_shape=jax.ShapeDtypeStruct(shape, BF16),
            compiler_params=params(),
            cost_estimate=cost(2),
            name="other_core_rows",
        )(place, forcing, after)

    def partner(values):
        return lax.ppermute(values, "rad", [(0, 1), (1, 0)])

    places = tuple(range(chips))
    every = tuple(range(own_modes))
    head, tail = every[: own_modes // 2], every[own_modes // 2 :]
    steps = [
        ("rows", 0, None),
        ("rows", 1, None),
        ("encode", 0, places),
        ("rows", 2, None),
        ("encode", 1, places),
        ("gather", 0, None),
        ("encode", 2, places),
        ("gather", 1, None),
        ("join", 0, None),
        ("gather", 2, None),
        ("join", 1, None),
        ("solve", 0, every),
        ("join", 2, None),
        ("solve", 1, every),
        ("finish", 0, every),
        ("solve", 2, head),
        ("solve", 2, tail),
        ("finish", 1, every),
        ("finish", 2, head),
        ("finish", 2, tail),
    ]
    swapped, own, away, spectra, partners = {}, {}, {}, {}, {}
    windows = {field: {} for field in range(fields)}
    last, out = diffusion, None
    for name, field, which in steps:
        key = (field, which)
        if name == "rows":
            last = other_rows(field, last)
            swapped[field] = flip(last, 1)
        elif name == "encode":
            made = encode(field, which, swapped[field], last)
            last = made[0]
            for target, message in zip(which, made):
                windows[field][target] = flip(message, 2 * target) if target else message
        elif name == "gather":
            own[field], last = gather([windows[field][j] for j in range(chips)], last)
            away[field] = flip(last, near)
        elif name == "join":
            last = join(own[field], away[field], last)
            spectra[field] = exchange(last, ("modes", "rad"), side_owners)
        elif name == "solve":
            out, last = solve(field, which, spectra[field], out, last)
            partners[key] = partner(last)
        else:
            out = finish(field, which, partners[key], out, last)
    return out


def azimuthal_tables(retained, points):
    row_index = jnp.arange(2 * retained, dtype=jnp.int32)
    wavenumber = row_index // 2
    quarter = (row_index % 2).astype(jnp.float32) * (0.5 * math.pi)
    theta_index = jnp.arange(points, dtype=jnp.int32)
    phase_index = wavenumber[:, None] * theta_index[None, :] % points
    radians = phase_index.astype(jnp.float32) * (2.0 * math.pi / points) + quarter[:, None]
    table = jnp.cos(radians) * (1.0 / math.sqrt(points))
    upper = table.astype(jnp.bfloat16)
    widened = lax.optimization_barrier(upper).astype(jnp.float32)
    lower = (table - widened).astype(jnp.bfloat16)
    return (upper, lower)


def modal_solve(spectral_coefficients, forward_map, backward, eigenvalues, axial_part, diffusion):
    highest_mode = lax.Precision.HIGHEST
    radial_coefficients = jnp.einsum(
        "hzv,bhtvp->bhtzp", forward_map, spectral_coefficients, precision=highest_mode
    )
    denominator = 1.0 + diffusion[:, None, None, None, None] * (
        eigenvalues[None, :, None, :, None] + axial_part[None, None, None, None, :]
    )
    return jnp.einsum(
        "mri,fmciq->fmcrq", backward, radial_coefficients / denominator, precision=highest_mode
    )


def general_plan(
    forcing,
    diffusion,
    axial_forward,
    axial_inverse_map,
    axial_eigenvalues,
    radial_forward,
    radial_backward,
    radial_eigenvalues,
):
    highest_mode = lax.Precision.HIGHEST
    fields, slab_points, radial_block, axial_points = forcing.shape
    mode_processors = lax.axis_size("modes")
    radial_devices = lax.axis_size("rad")
    total_theta = slab_points * mode_processors
    retained = radial_forward.shape[0] * mode_processors * radial_devices
    table_upper, table_lower = azimuthal_tables(retained, total_theta)
    flat_values = forcing.reshape(fields, slab_points, radial_block * axial_points)
    columns = lax.all_to_all(flat_values, "modes", split_axis=2, concat_axis=1, tiled=True)
    first = jnp.einsum("kt,ftc->fkc", table_upper, columns, preferred_element_type=jnp.float32)
    second = jnp.einsum("kt,ftc->fkc", table_lower, columns, preferred_element_type=jnp.float32)
    spectral = lax.all_to_all(first + second, "modes", split_axis=1, concat_axis=2, tiled=True)
    local_modes = spectral.shape[1] // 2
    spectral = spectral.reshape(fields, local_modes, 2, radial_block, axial_points)
    axial_coef = jnp.einsum("fmcrz,qz->fmcrq", spectral, axial_forward, precision=highest_mode)
    exchanged = lax.all_to_all(axial_coef, "rad", split_axis=4, concat_axis=3, tiled=True)
    forward_rows, backward_rows, eigen_rows = (
        lax.all_gather(radial_forward, "rad", axis=0, tiled=True),
        lax.all_gather(radial_backward, "rad", axis=0, tiled=True),
        lax.all_gather(radial_eigenvalues, "rad", axis=0, tiled=True),
    )
    axial_block = axial_points // radial_devices
    axial_part = lax.dynamic_slice_in_dim(
        axial_eigenvalues, lax.axis_index("rad") * axial_block, axial_block
    )
    solved = modal_solve(exchanged, forward_rows, backward_rows, eigen_rows, axial_part, diffusion)
    returned = lax.all_to_all(solved, "rad", split_axis=3, concat_axis=4, tiled=True)
    return jnp.einsum("fmcrq,zq->fmcrz", returned, axial_inverse_map, precision=highest_mode)


def per_device(forcing, diffusion, axial_forward, *maps):
    processors, radial_devices = lax.axis_size("modes"), lax.axis_size("rad")
    _, slab, radial_block, width = forcing.shape
    own_modes = maps[2].shape[0]
    paired = (
        radial_devices == 2
        and processors >= 8
        and processors & (processors - 1) == 0
        and radial_block == 8 * processors
        and width % 128 == 0
        and own_modes == 4
        and slab % 32 == 0
        and slab * processors == 8 * own_modes * processors * radial_devices
    )
    plan = paired_plan if paired else general_plan
    return plan(forcing, diffusion, axial_forward, *maps)


def solution(mesh):
    in_specs = (
        P(None, "modes", "rad", None),
        P(),
        P(),
        P(),
        P(),
        P(("modes", "rad"), None, None),
        P(("modes", "rad"), None, None),
        P(("modes", "rad"), None),
    )
    out_specs = P(None, "modes", None, "rad", None)
    return jax.shard_map(
        per_device, mesh=mesh, in_specs=in_specs, out_specs=out_specs, check_vma=False
    )
```
